512 devices in a mesh: grp: 16 (over z), dev: 32 (over x, y, core).
Axes of the slice: x: 4, y: 4, z: 16, core: 2. Of those that a mesh axis runs over, the one named last changes fastest.
Arguments:
- proj: bfloat16 [65536, 4096], P(('grp', 'dev')), may hold values from -6 to 6
- resid: bfloat16 [65536, 1024], P(('grp', 'dev')), may hold values from -6 to 6
- send_rows: int32 [512, 256], P(('grp', 'dev')), may hold values from 0 to 128, as said below
- pack_rows: int32 [512, 128], P(('grp', 'dev')), may hold values from 0 to 255, as said below
- segments: int32 [512, 128], P(('grp', 'dev')), may hold values from 0 to 3, never falling along the last dimension, each value on 1 to 64 neighbouring positions
- targets: int32 [512, 128], P(('grp', 'dev')), may hold values from 0 to 511
- ratios: float32 [512, 128], P(('grp', 'dev')), may hold values from 0.1 to 40
- negatives: int32 [16, 256], P('grp'), may hold values from 0 to 511
- table: bfloat16 [8192, 1024], P(('grp', 'dev')), may hold values from -6 to 6
- out_weight: bfloat16 [1024, 1024], P('dev'), may hold values from -0.1875 to 0.1875
- topk: int32 [1], replicated, may hold values from 2 to 16
Outputs:
- loss: float32 [1], replicated
- d_proj: bfloat16 [65536, 4096], P(('grp', 'dev'))
- d_table: float32 [8192, 1024], P(('grp', 'dev'))
The draws below stay inside these ranges and needn't reach their ends.
Inputs may be any that keep to these rules, and one draw needn't show every extreme that they name: `send_rows`: A device's slots name, for each of its 32 peers in turn, 8 slots holding distinct arrival rows of that device sent to that peer, then 128 in each unused slot; every arrival row is sent exactly once and every device receives 128 rows; in every group some device fills all 8 slots to one peer. `pack_rows`: each device's packed rows name distinct used received slots, numbered source member times 8 plus the place in that source's slots.
All inputs are finite; a program needn't handle non-finite values.
Results may differ from the reference program's by a relative error of at most 0.022.
Values may be sent and summed in bfloat16 or wider, within the bound.
No kernel may reach another device: no remote copies, remote signals or barrier semaphores. Data moves between devices by JAX's collectives and lax.ppermute only.
A program may use at most 64 MiB of HBM per device.

```python
import math
import jax
import jax.numpy as jnp
import numpy as np
from jax import lax

D = 1024
HEADS = 8
TOK_DEV = 128
ROWS = 65536
ITEMS = 512
NEG = 256
N_GRP = 16
N_DEV = 32
DEVICES = 512


def routing_tables(key):
    base_count = TOK_DEV // N_DEV
    capacity = 2 * base_count
    half_dev = N_DEV // 2
    group_keys = jax.random.split(key, N_GRP)

    def one_group(group_key):
        four_keys = jax.random.split(group_key, 3)
        offsets_half = jax.random.randint(four_keys[0], (half_dev, half_dev), -base_count, base_count + 1)
        offsets_half = offsets_half.at[0, 0].set(base_count)
        parity = jnp.arange(N_DEV) % 2
        sign_table = 1 - 2 * ((parity[:, None] + parity[None, :]) % 2)
        expand = jnp.arange(N_DEV) // 2
        counts = base_count + sign_table * offsets_half[expand[:, None], expand[None, :]]
        starts = jnp.cumsum(counts, axis=1) - counts
        arrival = jax.vmap(lambda sub_key: jax.random.permutation(sub_key, TOK_DEV))(jax.random.split(four_keys[1], N_DEV))
        slot_ids = jnp.arange(capacity)
        source_pos = starts[:, :, None] + slot_ids[None, None, :]
        occupied = slot_ids[None, None, :] < counts[:, :, None]
        clipped = jnp.minimum(source_pos, TOK_DEV - 1).reshape(N_DEV, N_DEV * capacity)
        picked = jnp.take_along_axis(arrival, clipped, axis=1).reshape(N_DEV, N_DEV, capacity)
        send_table = jnp.where(occupied, picked, TOK_DEV).reshape(N_DEV, N_DEV * capacity)
        used_recv = jnp.transpose(occupied, (1, 0, 2)).reshape(N_DEV, N_DEV * capacity)
        scores = jax.vmap(lambda sub_key: jax.random.permutation(sub_key, N_DEV * capacity))(jax.random.split(four_keys[2], N_DEV))
        ranked = jnp.where(used_recv, scores, scores + N_DEV * capacity)
        pack_table = jnp.argsort(ranked, axis=1, stable=True)[:, :TOK_DEV]
        return (send_table, pack_table)
    sends, packs = jax.vmap(one_group)(group_keys)
    return (sends.reshape(DEVICES, N_DEV * capacity).astype(jnp.int32), packs.reshape(DEVICES, TOK_DEV).astype(jnp.int32))


def common_signs(key):
    sign_key = jax.random.fold_in(key, 11)
    flips = jax.random.bernoulli(sign_key, 0.5, (N_GRP, D))
    return jnp.where(flips, 1.0, -1.0).astype(jnp.float32)


def draw_send_rows(key, part):
    tables = routing_tables(key)
    return tables[0]


def draw_pack_rows(key, part):
    tables = routing_tables(key)
    return tables[1]


def draw_ratios(key, part):
    key = jax.random.fold_in(key, 3)
    ranks = (jnp.arange(DEVICES * TOK_DEV) // TOK_DEV).astype(jnp.float32).reshape(DEVICES, TOK_DEV)
    spread = jnp.exp(jax.random.uniform(key, (DEVICES, TOK_DEV), jnp.float32, math.log(0.2), math.log(5.0)))
    rising = 1.0 + 2.0 * ranks / (DEVICES - 1)
    return spread * rising


def draw_resid(key, part):
    signs = common_signs(key)
    send_table = routing_tables(key)[0]
    key = jax.random.fold_in(key, 5)
    noise_key, jitter_key = jax.random.split(key)
    capacity = 2 * TOK_DEV // N_DEV
    slot_member = (jnp.arange(N_DEV * capacity) // capacity).astype(jnp.int32)

    def destination(row_ids):
        return jnp.zeros((TOK_DEV + 1,), jnp.int32).at[row_ids].set(slot_member)[:TOK_DEV]
    dest_member = jax.vmap(destination)(send_table)
    group_base = (jnp.arange(DEVICES) // N_DEV * N_DEV).astype(jnp.int32)
    dest_device = group_base[:, None] + dest_member
    ranks = jnp.arange(DEVICES).astype(jnp.float32) / (DEVICES - 1)
    noise = 0.8 * jax.random.normal(noise_key, (DEVICES, TOK_DEV, D), jnp.float32)
    jitter = jax.random.uniform(jitter_key, (DEVICES,), jnp.float32, 0.6, 1.4)
    strength = 1.2 * ranks * jitter
    row_strength = strength[dest_device]
    row_signs = signs[jnp.arange(DEVICES) // N_DEV]
    values = noise + row_strength[:, :, None] * row_signs[:, None, :]
    return jnp.clip(values, -6.0, 6.0).reshape(ROWS, D).astype(jnp.bfloat16)


def draw_table(key, part):
    signs = common_signs(key)
    key = jax.random.fold_in(key, 7)
    noise_key, lean_key = jax.random.split(key)
    noise = jax.random.normal(noise_key, (N_GRP * ITEMS, D), jnp.float32)
    lean = jax.random.uniform(lean_key, (N_GRP * ITEMS, 1), jnp.float32, -1.5, 1.5)
    row_signs = signs[jnp.arange(N_GRP * ITEMS) // ITEMS]
    return jnp.clip(noise + lean * row_signs, -6.0, 6.0).astype(jnp.bfloat16)


def touch_ends(result, stream_key, smallest, high):
    longest = result.shape.index(max(result.shape))
    spots = []
    for shift in (0, 1):
        where = [jax.random.randint(jax.random.fold_in(stream_key, axis), (), 0, length) for axis, length in enumerate(result.shape)]
        where[longest] = (where[longest] + shift) % result.shape[longest]
        spots.append(tuple(where))
    return result.at[spots[0]].set(smallest).at[spots[1]].set(high)


def block_levels(stream_key, dims, cuts, least, top_value):
    def one(axis_at, blocks):
        heights = jax.random.uniform(jax.random.fold_in(jax.random.fold_in(stream_key, 6), axis_at), (blocks,), jnp.float32, least / len(cuts), top_value / len(cuts))
        return jnp.repeat(jnp.exp(heights), dims[axis_at] // blocks).reshape((-1,) + (1,) * (len(dims) - axis_at - 1))

    level = one(*cuts[0])
    for cut in cuts[1:]:
        level = level * one(*cut)
    return level


def profile(number_of, total, most, skew):
    portions = [(1 << 20) // math.isqrt(standing ** skew) + 1 for standing in range(2, number_of + 1)]
    rest, given = total - most - (number_of - 1), [1] * (number_of - 1)
    while rest > 0:
        free = [i for i in range(number_of - 1) if given[i] < most]
        mass, left = sum([portions[i] for i in free]), rest
        for i in free:
            addition = min(most - given[i], max(1, left * portions[i] // mass), rest)
            given[i] = given[i] + addition
            rest = rest - addition
    return np.array([most] + given)


def ragged(key, amount, total, limit, skew):
    if amount == 2:
        one = jax.random.randint(key, (), max(1, total - limit), min(limit, total - 1) + 1)
        return jnp.stack([one, total - one])
    sizes = jnp.asarray(profile(amount, total, limit, skew), jnp.int32)
    couples = (amount - 1) // 2
    giver, sink = sizes[1:1 + 2 * couples:2], sizes[2:2 + 2 * couples:2]
    room = jnp.minimum(giver - 1, limit - sink)
    passed = jax.random.randint(jax.random.fold_in(key, 1), (couples,), 0, 1 << 20) % (room + 1)
    sizes = sizes.at[1:1 + 2 * couples:2].set(giver - passed).at[2:2 + 2 * couples:2].set(sink + passed)
    return sizes[jax.random.permutation(jax.random.fold_in(key, 2), amount)]


def gaussian(rng, dims, scale, most, pieces=(), kind=jnp.bfloat16):
    factor_of = block_levels(rng, dims, pieces, -0.22, 0.18) if pieces else 1.0
    result = jax.random.normal(rng, dims, jnp.float32) * scale * factor_of
    return jnp.minimum(jnp.maximum(result, -most), most).astype(kind)


def setup_inputs(seed: int = 0) -> dict:
    key_of = jax.random.split(jax.random.key(seed), 12)
    return {
        "proj": gaussian(key_of[0], (ROWS, 4 * D), 1.0, 6.0, ((0, 512),)),
        "resid": draw_resid(jax.random.fold_in(key_of[11], 71), 0),
        "send_rows": draw_send_rows(jax.random.fold_in(key_of[11], 71), 0),
        "pack_rows": draw_pack_rows(jax.random.fold_in(key_of[11], 71), 0),
        "segments": jax.vmap(lambda own: jnp.searchsorted(jnp.cumsum(ragged(own, 4, TOK_DEV, TOK_DEV // 2, 2)), jnp.arange(TOK_DEV), side="right"))(jax.random.split(key_of[4], DEVICES)).reshape((DEVICES, TOK_DEV)).astype(jnp.int32),
        "targets": touch_ends(jax.random.randint(key_of[5], (DEVICES, TOK_DEV), 0, ITEMS), jax.random.fold_in(key_of[5], 1), 0, ITEMS - 1).astype(jnp.int32),
        "ratios": draw_ratios(jax.random.fold_in(key_of[11], 71), 0),
        "negatives": touch_ends(jax.random.randint(key_of[7], (N_GRP, NEG), 0, ITEMS), jax.random.fold_in(key_of[7], 1), 0, ITEMS - 1).astype(jnp.int32),
        "table": draw_table(jax.random.fold_in(key_of[11], 71), 0),
        "out_weight": gaussian(key_of[9], (D, D), D ** -0.5, 0.1875, ((0, 32),)),
        "topk": jax.random.randint(key_of[10], (1,), 2, 17).astype(jnp.int32),
    }


sharpness = 20.0

def rounded(values):
    return lax.optimization_barrier(values.astype(jnp.bfloat16))

def silu_grad(values):
    logistic = jax.nn.sigmoid(values)
    return logistic * (1.0 + values * (1.0 - logistic))

def device_pass(pre_rows, resid_rows, segment, target, ratio, item_bf, counts, weight_full, topk_value, total_ratio):
    token_count = pre_rows.shape[0]
    model_width = weight_full.shape[0]
    pre_act = pre_rows.astype(jnp.float32)
    activated = jax.nn.silu(pre_act)
    act_bf = rounded(activated)
    gate_u = activated[:, :model_width]
    value_h = act_bf[:, model_width:2 * model_width].reshape(token_count, HEADS, -1).astype(jnp.float32)
    query_h = act_bf[:, 2 * model_width:3 * model_width].reshape(token_count, HEADS, -1).astype(jnp.float32)
    key_h = act_bf[:, 3 * model_width:].reshape(token_count, HEADS, -1).astype(jnp.float32)
    head_dim = value_h.shape[2]
    scaling = head_dim ** (-0.5)
    norm_len = token_count // 2
    positions = jnp.arange(token_count)
    causal_mask = (segment[:, None] == segment[None, :]) & (positions[None, :] <= positions[:, None])
    scores = jnp.einsum('ihd,jhd->hij', query_h, key_h) * scaling
    attention = jnp.where(causal_mask[None], jax.nn.silu(scores), 0.0) / norm_len
    att_f = rounded(attention).astype(jnp.float32)
    mixed = jnp.einsum('hij,jhd->ihd', att_f, value_h).reshape(token_count, model_width)
    row_mean = lax.optimization_barrier(jnp.mean(mixed, 1, keepdims=True))
    centered = mixed - row_mean
    inv_dev = lax.rsqrt(lax.optimization_barrier(jnp.mean(centered * centered, 1, keepdims=True)) + 1e-05)
    normed = centered * inv_dev
    gated_bf = rounded(normed * gate_u)
    output = resid_rows.astype(jnp.float32) + jnp.dot(gated_bf, weight_full, preferred_element_type=jnp.float32)
    inv_out = lax.rsqrt(lax.optimization_barrier(jnp.sum(output * output, 1, keepdims=True)) + 1e-06)
    user = output * inv_out
    user_bf = rounded(user)
    logits = sharpness * jnp.dot(user_bf, item_bf.T, preferred_element_type=jnp.float32)
    item_ids = jnp.arange(logits.shape[1])
    onehot = (target[:, None] == item_ids[None, :]).astype(jnp.float32)
    weighted = counts[None, :] + onehot
    exponent = jnp.exp(logits)
    totals = lax.optimization_barrier(jnp.sum(weighted * exponent, 1))
    positive = lax.optimization_barrier(jnp.sum(onehot * logits, 1))
    target_prob = jnp.exp(positive) / totals
    row_loss = jnp.log(totals) - positive
    correction = topk_value * jnp.power(1.0 - target_prob, topk_value - 1.0)
    row_weight = ratio * correction
    numerator = jnp.sum(row_weight * row_loss)
    row_coef = row_weight / total_ratio
    d_logits = row_coef[:, None] * (weighted * exponent / totals[:, None] - onehot)
    grad_bf = rounded(sharpness * d_logits)
    d_user = jnp.dot(grad_bf, item_bf, preferred_element_type=jnp.float32)
    d_item = jnp.dot(grad_bf.T, user_bf, preferred_element_type=jnp.float32)
    d_output = inv_out * (d_user - user * lax.optimization_barrier(jnp.sum(user * d_user, 1, keepdims=True)))
    dout_bf = rounded(d_output)
    d_gated = jnp.dot(dout_bf, weight_full.T, preferred_element_type=jnp.float32)
    d_normed = d_gated * gate_u
    d_gate = d_gated * normed
    d_mixed = inv_dev * (d_normed - lax.optimization_barrier(jnp.mean(d_normed, 1, keepdims=True)) - normed * lax.optimization_barrier(jnp.mean(d_normed * normed, 1, keepdims=True)))
    dmix_f = rounded(d_mixed).reshape(token_count, HEADS, -1).astype(jnp.float32)
    d_att = jnp.einsum('ihd,jhd->hij', dmix_f, value_h)
    d_value = jnp.einsum('hij,ihd->jhd', att_f, dmix_f)
    d_scores = rounded(jnp.where(causal_mask[None], d_att * silu_grad(scores), 0.0) * (scaling / norm_len)).astype(jnp.float32)
    d_query = jnp.einsum('hij,jhd->ihd', d_scores, key_h)
    d_key = jnp.einsum('hij,ihd->jhd', d_scores, query_h)
    d_act = jnp.concatenate([d_gate, d_value.reshape(token_count, model_width), d_query.reshape(token_count, model_width), d_key.reshape(token_count, model_width)], 1)
    d_pre = (d_act * silu_grad(pre_act)).astype(jnp.bfloat16)
    return (numerator, d_pre, d_item)

def reference(proj, resid, send_rows, pack_rows, segments, targets, ratios, negatives, table, out_weight, topk):
    capacity = 2 * TOK_DEV // N_DEV
    device_ids = jnp.arange(DEVICES, dtype=jnp.int32)
    group_of = device_ids // N_DEV
    member = device_ids % N_DEV
    source = group_of[:, None] * N_DEV + pack_rows // capacity
    slot_in = member[:, None] * capacity + pack_rows % capacity
    arrival = send_rows[source, slot_in]
    global_row = (source * TOK_DEV + arrival).astype(jnp.int32).reshape(N_GRP, N_DEV * TOK_DEV)
    total_ratio = jnp.sum(ratios)
    topk_value = topk[0].astype(jnp.float32)
    table_groups = table.reshape(N_GRP, ITEMS, D)

    def one_group(packed):
        rows_g, seg_g, tgt_g, ratio_g, neg_g, table_g = packed
        pre_g = jnp.take(proj, rows_g, axis=0).reshape(N_DEV, TOK_DEV, 4 * D)
        resid_g = jnp.take(resid, rows_g, axis=0).reshape(N_DEV, TOK_DEV, D)
        tab_rows = table_g.astype(jnp.float32)
        inv_tab = lax.rsqrt(lax.optimization_barrier(jnp.sum(tab_rows * tab_rows, 1, keepdims=True)) + 1e-06)
        item = tab_rows * inv_tab
        item_bf = rounded(item)
        item_ids = jnp.arange(ITEMS)
        counts = lax.optimization_barrier(jnp.sum((neg_g[:, None] == item_ids[None, :]).astype(jnp.float32), 0))

        def per_device(pre_rows, resid_rows, segment, target, ratio):
            return device_pass(pre_rows, resid_rows, segment, target, ratio, item_bf, counts, out_weight, topk_value, total_ratio)
        numerators, d_pre, d_items = jax.vmap(per_device)(pre_g, resid_g, seg_g, tgt_g, ratio_g)
        summed = lax.optimization_barrier(jnp.sum(d_items, 0))
        d_tab = inv_tab * (summed - item * lax.optimization_barrier(jnp.sum(item * summed, 1, keepdims=True)))
        return (jnp.sum(numerators), d_pre, d_tab)
    numerators, d_pre, d_tab = lax.map(one_group, (global_row, segments.reshape(N_GRP, N_DEV, TOK_DEV), targets.reshape(N_GRP, N_DEV, TOK_DEV), ratios.reshape(N_GRP, N_DEV, TOK_DEV), negatives, table_groups))
    loss = (jnp.sum(numerators) / total_ratio).reshape(1)
    return (loss, d_pre.reshape(ROWS, 4 * D), d_tab.reshape(N_GRP * ITEMS, D))
```

```python
import jax
import jax.numpy as jnp
from jax import lax
from jax.experimental import pallas as pl
from jax.experimental.pallas import tpu as pltpu
from jax.sharding import Mesh, PartitionSpec as P

HEADS = 8
SHARP = 20.0
BF = jnp.bfloat16
F32 = jnp.float32
MEMBERS = ("x", "y", "c")
EVERY = ("z", "x", "y", "c")
PLANES = 4
SHIFTS = (0, 1, -1, 2)
PARAMS = dict(vmem_limit_bytes=32 * 1024 * 1024)


def dot_nn(a, b):
    return lax.dot_general(a, b, (((1,), (0,)), ((), ())), preferred_element_type=F32)


def dot_nt(a, b):
    return lax.dot_general(a, b, (((1,), (1,)), ((), ())), preferred_element_type=F32)


def dot_tn(a, b):
    return lax.dot_general(a, b, (((0,), (0,)), ((), ())), preferred_element_type=F32)


def sigmoid(values):
    return 1.0 / (1.0 + jnp.exp(-values))


def as_column(row):
    n = row.shape[1]
    return jnp.broadcast_to(row, (n, n)).T[:, :1]


def vmem(count):
    return [pl.BlockSpec(memory_space=pltpu.VMEM)] * count


def estimate(flops, nbytes, trans=0):
    return pl.CostEstimate(flops=flops, bytes_accessed=nbytes, transcendentals=trans)


def hbm(count):
    return [pl.BlockSpec(memory_space=pltpu.HBM)] * count


def in_hbm(*arrays):
    return [pltpu.with_memory_space_constraint(a, pltpu.HBM) for a in arrays]


def send_kernel(slots_in, proj_in, resid_in, out_ref, slots_ref, rows_ref, send_ref, in_sems, out_sems):
    rows, width = resid_in.shape
    slots = slots_ref.shape[1]
    parts = [slice(n * width, (n + 1) * width) for n in range(5)]
    first = pltpu.make_async_copy(slots_in, slots_ref, in_sems.at[5])
    first.start()
    into = []
    for n, part in enumerate(parts):
        source = resid_in if n == 4 else proj_in.at[:, part]
        into.append(pltpu.make_async_copy(source, rows_ref.at[:, part], in_sems.at[n]))
        into[-1].start()
    first.wait()
    ids = lax.broadcasted_iota(jnp.int32, (rows, slots), 0)
    pick = (ids == slots_ref[...]).astype(F32).T.astype(BF)
    out = []
    for n, part in enumerate(parts):
        into[n].wait()
        send_ref[:, part] = dot_nn(pick, rows_ref[:, part]).astype(BF)
        out.append(pltpu.make_async_copy(send_ref.at[:, part], out_ref.at[:, part], out_sems.at[n]))
        out[-1].start()
    for copy in out:
        copy.wait()


def send_blocks(slots, proj, resid):
    rows, width = resid.shape
    count = slots.shape[1]
    return pl.pallas_call(
        send_kernel,
        in_specs=hbm(3),
        out_specs=hbm(1)[0],
        out_shape=pltpu.HBM((count, 5 * width), BF),
        scratch_shapes=[
            pltpu.VMEM((1, count), jnp.int32),
            pltpu.VMEM((rows, 5 * width), BF),
            pltpu.VMEM((count, 5 * width), BF),
            pltpu.SemaphoreType.DMA((6,)),
            pltpu.SemaphoreType.DMA((5,)),
        ],
        compiler_params=pltpu.CompilerParams(**PARAMS),
        cost_estimate=estimate(2 * count * rows * 5 * width, 2 * 5 * width * (rows + count)),
        name="send_blocks",
    )(*in_hbm(slots, proj, resid))


def shared_kernel(table_in, weight_in, out_ref, table_ref, weight_ref, send_ref, sems):
    width = table_in.shape[1]
    size = weight_ref.shape[1]
    half = width // 2
    first = lax.rem(lax.axis_index("z"), width // size) * size
    into = [
        pltpu.make_async_copy(
            weight_in.at[:, pl.ds(pl.multiple_of(first, size), size)], weight_ref, sems.at[0]
        ),
        pltpu.make_async_copy(table_in, table_ref, sems.at[1]),
    ]
    for copy in into:
        copy.start()
    for copy in into:
        copy.wait()
    weight = weight_ref[...]
    table = table_ref[...].astype(F32)
    left, right = table[:, :half], table[:, half:]
    narrow = jnp.concatenate([left[:8], right[:8], left[8:], right[8:]], 0).astype(BF)
    for tile in range(send_ref.shape[0] // 32):
        send_ref[tile * 32 : (tile + 1) * 32, :size] = weight
        send_ref[tile * 32 : (tile + 1) * 32, size:] = narrow
    back = pltpu.make_async_copy(send_ref, out_ref, sems.at[2])
    back.start()
    back.wait()


def shared_blocks(table, weight, members):
    width = table.shape[1]
    size = width // PLANES
    shape = (members * 16, size + width // 2)
    return pl.pallas_call(
        shared_kernel,
        in_specs=hbm(2),
        out_specs=hbm(1)[0],
        out_shape=pltpu.HBM(shape, BF),
        scratch_shapes=[
            pltpu.VMEM(table.shape, BF),
            pltpu.VMEM((weight.shape[0], size), BF),
            pltpu.VMEM(shape, BF),
            pltpu.SemaphoreType.DMA((3,)),
        ],
        compiler_params=pltpu.CompilerParams(**PARAMS),
        cost_estimate=estimate(2 * shape[0] * shape[1], 2 * shape[0] * shape[1]),
        name="shared_blocks",
    )(*in_hbm(table, weight))


def weight_copies(near_in, far_in, weight_ref, sems):
    width = weight_ref.shape[3]
    size = width // PLANES
    z, core = lax.axis_index("z"), lax.axis_index("c")
    copies = []
    for source, side in ((near_in, core), (far_in, 1 - core)):
        for n, shift in enumerate(SHIFTS):
            first = pl.multiple_of(lax.rem(z + shift + PLANES, PLANES) * size, size)
            copies.append(
                pltpu.make_async_copy(
                    source.at[:, :, n * size : (n + 1) * size],
                    weight_ref.at[:, side, :, pl.ds(first, size)],
                    sems.at[len(copies)],
                )
            )
    return copies


def causal_mask(segment_row):
    n = segment_row.shape[1]
    spread = jnp.broadcast_to(segment_row.astype(F32), (n, n))
    rows = lax.broadcasted_iota(jnp.int32, (n, n), 0)
    cols = lax.broadcasted_iota(jnp.int32, (n, n), 1)
    return (spread == spread.T) & (cols <= rows)


def in_pieces(value):
    high = value.astype(BF).astype(F32)
    middle = (value - high).astype(BF).astype(F32)
    return high, middle, value - high - middle


def forward_kernel(
    order_ref, segments_ref, got_ref, near_in, far_in, negatives_ref, targets_ref, ratios_ref,
    topk_ref,
    grad_ref, invd_ref, inv_ref, ditem_out, user_out, item_out, pre_out, normed_out,
    pre_ref, normed_ref, resid_ref, ditem_ref, user_ref, item_ref, weight_ref, near_ref, far_ref,
    in_sems, out_sems,
):
    slots = got_ref.shape[0]
    rows, width = normed_ref.shape
    items = item_ref.shape[0]
    head = width // HEADS
    half = width // 2
    into = weight_copies(near_in, far_in, weight_ref, in_sems)
    into += [
        pltpu.make_async_copy(near_in.at[:, :, width:], near_ref, in_sems.at[2 * PLANES]),
        pltpu.make_async_copy(far_in.at[:, :, width:], far_ref, in_sems.at[2 * PLANES + 1]),
    ]
    for copy in into:
        copy.start()
    ids = lax.broadcasted_iota(jnp.int32, (slots, rows), 0)
    pick = (ids == order_ref[...]).astype(F32).T.astype(BF)
    for part in range(4):
        columns = slice(part * width, (part + 1) * width)
        pre_ref[:, columns] = dot_nn(pick, got_ref[:, columns]).astype(BF)
    resid_ref[...] = dot_nn(pick, got_ref[:, 4 * width :])
    save_pre = pltpu.make_async_copy(pre_ref, pre_out, out_sems.at[6])
    save_pre.start()
    mask = causal_mask(segments_ref[...])
    scaling = head ** (-0.5)

    def activated(part, h):
        start = part * width + h * head
        values = pre_ref[:, start : start + head].astype(F32)
        return values * sigmoid(values)

    for h in range(HEADS):
        value_h = activated(1, h).astype(BF)
        query_h = activated(2, h).astype(BF)
        key_h = activated(3, h).astype(BF)
        scores = dot_nt(query_h, key_h) * scaling
        att = jnp.where(mask, scores * sigmoid(scores), 0.0) * (2.0 / rows)
        normed_ref[:, h * head : (h + 1) * head] = dot_nn(att.astype(BF), value_h)
    mixed = normed_ref[...]
    centered = mixed - jnp.mean(mixed, 1, keepdims=True)
    inv_dev = lax.rsqrt(jnp.mean(centered * centered, 1, keepdims=True) + 1e-05)
    normed = centered * inv_dev
    normed_ref[...] = normed
    save_normed = pltpu.make_async_copy(normed_ref, normed_out, out_sems.at[7])
    save_normed.start()
    invd_ref[...] = inv_dev
    gate = pre_ref[:, :width].astype(F32)
    gated = (normed * (gate * sigmoid(gate))).astype(BF)
    for copy in into:
        copy.wait()
    weight = weight_ref[...].reshape(width, width)
    output = resid_ref[...] + dot_nn(gated, weight)
    inverse = lax.rsqrt(jnp.sum(output * output, 1, keepdims=True) + 1e-06)
    user = output * inverse
    user_ref[...] = user
    save_user = pltpu.make_async_copy(user_ref, user_out, out_sems.at[0])
    save_user.start()
    inv_ref[...] = inverse
    user_bf = user.astype(BF)
    drawn = negatives_ref.shape[1]
    hits = (lax.broadcasted_iota(jnp.int32, (items, drawn), 0) == negatives_ref[...]).astype(F32)
    counts = dot_nt(jnp.ones((8, drawn), BF), hits.astype(BF))[:1]
    ids = lax.broadcasted_iota(jnp.int32, (rows, items), 1)
    target = as_column(targets_ref[...].astype(F32)).astype(jnp.int32)
    onehot = jnp.where(ids == target, 1.0, 0.0)
    first = lax.axis_index("c") == 0
    near = near_ref[...].astype(F32)
    far = far_ref[...].astype(F32)
    near = jnp.concatenate([near[:, :8], near[:, 8:]], 2)
    far = jnp.concatenate([far[:, :8], far[:, 8:]], 2)
    low = jnp.where(first, near, far)
    high = jnp.where(first, far, near)
    values = jnp.concatenate([low, high], 1).reshape(items, width)
    item_inv = lax.rsqrt(jnp.sum(values * values, 1, keepdims=True) + 1e-06)
    item_ref[...] = (values * item_inv).astype(BF)
    save_item = pltpu.make_async_copy(item_ref, item_out, out_sems.at[1])
    save_item.start()
    logits = SHARP * dot_nt(user_bf, item_ref[...])
    mass = (counts + onehot) * jnp.exp(logits)
    totals = jnp.sum(mass, 1, keepdims=True)
    positive = jnp.sum(onehot * logits, 1, keepdims=True)
    rest = 1.0 - jnp.exp(positive) / totals
    row_loss = jnp.log(totals) - positive
    size = topk_ref[0]
    power = jnp.ones_like(rest)
    square = rest
    for bit in range(4):
        power = jnp.where((((size - 1) >> bit) & 1) == 1, power * square, power)
        square = square * square
    ratio = as_column(ratios_ref[...])
    row_weight = ratio * (size.astype(F32) * power)
    grad = (SHARP * row_weight) * (mass / totals - onehot)
    grad_bf = grad.astype(BF)
    grad_ref[...] = grad_bf
    numerator = jnp.sum(row_weight * row_loss, 0, keepdims=True)
    lanes = lax.broadcasted_iota(jnp.int32, (items, 128), 1)
    extra = jnp.zeros((items, 128), F32)
    pieces = in_pieces(numerator) + in_pieces(jnp.sum(ratio, 0, keepdims=True))
    for lane, piece in enumerate(pieces):
        extra = jnp.where(lanes == lane, piece, extra)
    ditem_ref[:, width:] = extra.astype(BF)
    out = []
    steps = 4
    for step in range(steps):
        at = slice(step * items // steps, (step + 1) * items // steps)
        ditem_ref[at, :width] = dot_tn(grad_bf[:, at], user_bf).astype(BF)
        out.append(
            pltpu.make_async_copy(ditem_ref.at[at, :], ditem_out.at[at, :], out_sems.at[2 + step])
        )
        out[-1].start()
    for copy in [save_user, save_item, save_pre, save_normed] + out:
        copy.wait()


def forward_pass(order, segments, got, near, far, negatives, targets, ratios, topk):
    rows = order.shape[1]
    width = got.shape[1] // 5
    members, block = near.shape[:2]
    items = members * block
    return pl.pallas_call(
        forward_kernel,
        in_specs=vmem(3) + hbm(2) + vmem(3) + [pl.BlockSpec(memory_space=pltpu.SMEM)],
        out_specs=vmem(3) + hbm(5),
        out_shape=[
            jax.ShapeDtypeStruct((rows, items), BF),
            jax.ShapeDtypeStruct((rows, 1), F32),
            jax.ShapeDtypeStruct((rows, 1), F32),
            pltpu.HBM((items, width + 128), BF),
            pltpu.HBM((rows, width), F32),
            pltpu.HBM((items, width), BF),
            pltpu.HBM((rows, 4 * width), BF),
            pltpu.HBM((rows, width), F32),
        ],
        scratch_shapes=[
            pltpu.VMEM((rows, 4 * width), BF),
            pltpu.VMEM((rows, width), F32),
            pltpu.VMEM((rows, width), F32),
            pltpu.VMEM((items, width + 128), BF),
            pltpu.VMEM((rows, width), F32),
            pltpu.VMEM((items, width), BF),
            pltpu.VMEM((members, 2, block, width), BF),
            pltpu.VMEM((members, block, width // 2), BF),
            pltpu.VMEM((members, block, width // 2), BF),
            pltpu.SemaphoreType.DMA((2 * PLANES + 2,)),
            pltpu.SemaphoreType.DMA((8,)),
        ],
        compiler_params=pltpu.CompilerParams(**PARAMS),
        cost_estimate=estimate(2 * rows * width * 3328, 12 * 1024 * 1024),
        name="forward_pass",
    )(order, segments, got, *in_hbm(near, far), negatives, targets, ratios, topk)


def back_kernel(
    pre_ref, normed_ref, invd_ref, segments_ref, grad_ref, user_ref, invo_ref, item_ref, near_in, far_in,
    out_ref, weight_ref, sems,
):
    rows, width = normed_ref.shape
    head = width // HEADS
    into = weight_copies(near_in, far_in, weight_ref, sems)
    for copy in into:
        copy.start()
    user = user_ref[...]
    d_user = dot_nn(grad_ref[...], item_ref[...])
    d_output = invo_ref[...] * (d_user - user * jnp.sum(user * d_user, 1, keepdims=True))
    for copy in into:
        copy.wait()
    d_gated = dot_nt(d_output.astype(BF), weight_ref[...].reshape(width, width))
    normed = normed_ref[...]
    gate = pre_ref[:, :width].astype(F32)
    gate_s = sigmoid(gate)
    d_normed = d_gated * (gate * gate_s)
    d_gate = d_gated * normed
    out_ref[:, :width] = d_gate * (gate_s * (1.0 + gate * (1.0 - gate_s)))
    d_mixed = invd_ref[...] * (
        d_normed
        - jnp.mean(d_normed, 1, keepdims=True)
        - normed * jnp.mean(d_normed * normed, 1, keepdims=True)
    )
    dmix_bf = d_mixed.astype(BF)
    mask = causal_mask(segments_ref[...])
    scaling = head ** (-0.5)

    def opened(part, h):
        start = part * width + h * head
        values = pre_ref[:, start : start + head].astype(F32)
        logistic = sigmoid(values)
        slope = logistic * (1.0 + values * (1.0 - logistic))
        return (values * logistic).astype(BF), slope

    for h in range(HEADS):
        value_h, value_slope = opened(1, h)
        query_h, query_slope = opened(2, h)
        key_h, key_slope = opened(3, h)
        scores = dot_nt(query_h, key_h) * scaling
        logistic = sigmoid(scores)
        att = jnp.where(mask, scores * logistic, 0.0) * (2.0 / rows)
        dmix_h = dmix_bf[:, h * head : (h + 1) * head]
        d_att = dot_nt(dmix_h, value_h)
        d_value = dot_tn(att.astype(BF), dmix_h)
        slope = logistic * (1.0 + scores * (1.0 - logistic))
        d_scores = jnp.where(mask, d_att * slope, 0.0) * (scaling * 2.0 / rows)
        d_scores = d_scores.astype(BF)
        d_query = dot_nn(d_scores, key_h)
        d_key = dot_tn(d_scores, query_h)
        for part, grad, rate in (
            (1, d_value, value_slope), (2, d_query, query_slope), (3, d_key, key_slope)
        ):
            start = part * width + h * head
            out_ref[:, start : start + head] = grad * rate


def back_pass(pre, normed, inv_dev, segments, grad, user, inv_out, item, near, far):
    rows, width = normed.shape
    members, block = near.shape[:2]
    return pl.pallas_call(
        back_kernel,
        in_specs=vmem(8) + hbm(2),
        out_specs=pl.BlockSpec(memory_space=pltpu.VMEM),
        out_shape=jax.ShapeDtypeStruct((rows, 4 * width), F32),
        scratch_shapes=[
            pltpu.VMEM((members, 2, block, width), BF),
            pltpu.SemaphoreType.DMA((2 * PLANES,)),
        ],
        compiler_params=pltpu.CompilerParams(**PARAMS),
        cost_estimate=estimate(2 * rows * width * 2304, 8 * 1024 * 1024),
        name="back_pass",
    )(pre, normed, inv_dev, segments, grad, user, inv_out, item, *in_hbm(near, far))


def table_kernel(got_ref, table_ref, out_ref, sums_ref):
    width = table_ref.shape[1]
    summed = jnp.sum(got_ref[:, :, :width].astype(F32), 0)
    own = table_ref[...].astype(F32)
    inverse = lax.rsqrt(jnp.sum(own * own, 1, keepdims=True) + 1e-06)
    item = own * inverse
    inner = jnp.sum(item * summed, 1, keepdims=True)
    out_ref[...] = inverse * (summed - item * inner)
    extra = jnp.sum(got_ref[:, :, width:].astype(F32), 0)[:8]
    sums_ref[...] = jnp.broadcast_to(extra[None], sums_ref.shape)


def table_pass(got, table, groups):
    return pl.pallas_call(
        table_kernel,
        in_specs=vmem(2),
        out_specs=vmem(2),
        out_shape=[
            jax.ShapeDtypeStruct(table.shape, F32),
            jax.ShapeDtypeStruct((groups, 8, 128), F32),
        ],
        compiler_params=pltpu.CompilerParams(**PARAMS),
        cost_estimate=estimate(got.size * 2, got.size * 2),
        name="table_pass",
    )(got, table)


def finish_kernel(sums_ref, act_ref, table_ref, loss_ref, proj_out, out_ref, proj_ref, sems):
    row = jnp.sum(sums_ref[...], 0)[:1]
    lanes = lax.broadcasted_iota(jnp.int32, row.shape, 1)
    numerator = jnp.sum(jnp.where(lanes < 3, row, 0.0), 1, keepdims=True)
    total = jnp.sum(jnp.where(lanes < 3, 0.0, row), 1, keepdims=True)
    share = 1.0 / total
    steps = 4
    size = act_ref.shape[0] // steps
    out = []
    for step in range(steps):
        at = slice(step * size, (step + 1) * size)
        proj_ref[at, :] = (act_ref[at, :] * share).astype(BF)
        out.append(
            pltpu.make_async_copy(proj_ref.at[at, :], proj_out.at[at, :], sems.at[step])
        )
        out[-1].start()
    loss_ref[...] = jnp.broadcast_to(numerator * share, loss_ref.shape)
    out_ref[...] = table_ref[...] * share
    for copy in out:
        copy.wait()


def finish(sums, d_act, d_table):
    rows, columns = d_act.shape
    return pl.pallas_call(
        finish_kernel,
        in_specs=vmem(3),
        out_specs=vmem(1) + hbm(1) + vmem(1),
        out_shape=[
            jax.ShapeDtypeStruct((1, 128), F32),
            jax.ShapeDtypeStruct((rows, columns), BF),
            jax.ShapeDtypeStruct(d_table.shape, F32),
        ],
        scratch_shapes=[pltpu.VMEM((rows, columns), BF), pltpu.SemaphoreType.DMA((4,))],
        compiler_params=pltpu.CompilerParams(**PARAMS),
        cost_estimate=estimate(rows * columns, rows * columns * 6),
        name="finish",
    )(sums, d_act, d_table)


def shards(
    proj, resid, send_rows, pack_rows, segments, targets, ratios, negatives, table, out_weight, topk,
    *, groups, members,
):
    width = resid.shape[1]
    mine = table.shape[0]
    with jax.named_scope("shared"):
        share = shared_blocks(table, out_weight, members)
        share = lax.all_to_all(
            share.reshape(members, mine, share.shape[1]), MEMBERS, 0, 0, tiled=True
        )
    with jax.named_scope("route"):
        send = send_blocks(send_rows, proj, resid)
        got = lax.all_to_all(
            send.reshape(members, -1, 5 * width), MEMBERS, 0, 0, tiled=True
        ).reshape(send.shape)
    with jax.named_scope("planes"):
        size = width // PLANES
        mine_part = share[:, :, :size]
        parts = [mine_part]
        for shift in SHIFTS[1:]:
            pairs = [(i, (i - shift) % groups) for i in range(groups)]
            parts.append(lax.ppermute(mine_part, "z", pairs))
        near = jnp.concatenate(parts + [share[:, :, size:]], 2)
        far = lax.ppermute(near, "c", [(0, 1), (1, 0)])
    grad, inv_dev, inv_out, d_item, user, item, pre, normed = forward_pass(
        pack_rows, segments, got, near, far, negatives, targets, ratios, topk
    )
    with jax.named_scope("items_back"):
        got_item = lax.all_to_all(
            d_item.reshape(members, mine, width + 128), MEMBERS, 0, 0, tiled=True
        )
    d_act = back_pass(pre, normed, inv_dev, segments, grad, user, inv_out, item, near, far)
    d_table, sums = table_pass(got_item, table, groups)
    with jax.named_scope("sums"):
        sums = lax.all_to_all(sums, "z", 0, 0, tiled=True)
    loss, d_proj, d_table = finish(sums, d_act, d_table)
    return (loss[0, :1], d_proj, d_table)


def solution(mesh):
    groups, members = mesh.devices.shape
    side = 4
    fine = Mesh(
        mesh.devices.reshape(groups, side, members // (2 * side), 2), ("z", "x", "y", "c")
    )

    def body(*args):
        return shards(*args, groups=groups, members=members)

    return jax.shard_map(
        body,
        mesh=fine,
        in_specs=(
            P(EVERY, None),
            P(EVERY, None),
            P(EVERY, None),
            P(EVERY, None),
            P(EVERY, None),
            P(EVERY, None),
            P(EVERY, None),
            P("z", None),
            P(EVERY, None),
            P(MEMBERS, None),
            P(),
        ),
        out_specs=(P(), P(EVERY, None), P(EVERY, None)),
        check_vma=False,
    )
```

```python
import jax
import jax.numpy as jnp
from jax import lax
from jax.experimental import pallas as pl
from jax.experimental.pallas import tpu as pltpu
from jax.sharding import Mesh, PartitionSpec as P

HEADS = 8
SHARP = 20.0
BF = jnp.bfloat16
F32 = jnp.float32
MEMBERS = ("x", "y", "c")
EVERY = ("z", "x", "y", "c")
PLANES = 4
SHIFTS = (0, 1, -1, 2)
PARAMS = dict(vmem_limit_bytes=32 * 1024 * 1024)


def dot_nn(a, b):
    return lax.dot_general(a, b, (((1,), (0,)), ((), ())), preferred_element_type=F32)


def dot_nt(a, b):
    return lax.dot_general(a, b, (((1,), (1,)), ((), ())), preferred_element_type=F32)


def dot_tn(a, b):
    return lax.dot_general(a, b, (((0,), (0,)), ((), ())), preferred_element_type=F32)


def sigmoid(values):
    return 1.0 / (1.0 + jnp.exp(-values))


def as_column(row):
    n = row.shape[1]
    return jnp.broadcast_to(row, (n, n)).T[:, :1]


def vmem(count):
    return [pl.BlockSpec(memory_space=pltpu.VMEM)] * count


def estimate(flops, nbytes, trans=0):
    return pl.CostEstimate(flops=flops, bytes_accessed=nbytes, transcendentals=trans)


def hbm(count):
    return [pl.BlockSpec(memory_space=pltpu.HBM)] * count


def in_hbm(*arrays):
    return [pltpu.with_memory_space_constraint(a, pltpu.HBM) for a in arrays]


def send_kernel(slots_in, proj_in, resid_in, out_ref, slots_ref, rows_ref, send_ref, in_sems, out_sems):
    rows, width = resid_in.shape
    slots = slots_ref.shape[1]
    parts = [slice(n * width, (n + 1) * width) for n in range(5)]
    first = pltpu.make_async_copy(slots_in, slots_ref, in_sems.at[5])
    first.start()
    into = []
    for n, part in enumerate(parts):
        source = resid_in if n == 4 else proj_in.at[:, part]
        into.append(pltpu.make_async_copy(source, rows_ref.at[:, part], in_sems.at[n]))
        into[-1].start()
    first.wait()
    ids = lax.broadcasted_iota(jnp.int32, (rows, slots), 0)
    pick = (ids == slots_ref[...]).astype(F32).T.astype(BF)
    out = []
    for n, part in enumerate(parts):
        into[n].wait()
        send_ref[:, part] = dot_nn(pick, rows_ref[:, part]).astype(BF)
        out.append(pltpu.make_async_copy(send_ref.at[:, part], out_ref.at[:, part], out_sems.at[n]))
        out[-1].start()
    for copy in out:
        copy.wait()


def send_blocks(slots, proj, resid):
    rows, width = resid.shape
    count = slots.shape[1]
    return pl.pallas_call(
        send_kernel,
        in_specs=hbm(3),
        out_specs=hbm(1)[0],
        out_shape=pltpu.HBM((count, 5 * width), BF),
        scratch_shapes=[
            pltpu.VMEM((1, count), jnp.int32),
            pltpu.VMEM((rows, 5 * width), BF),
            pltpu.VMEM((count, 5 * width), BF),
            pltpu.SemaphoreType.DMA((6,)),
            pltpu.SemaphoreType.DMA((5,)),
        ],
        compiler_params=pltpu.CompilerParams(**PARAMS),
        cost_estimate=estimate(2 * count * rows * 5 * width, 2 * 5 * width * (rows + count)),
        name="send_blocks",
    )(*in_hbm(slots, proj, resid))


def shared_kernel(table_in, weight_in, out_ref, table_ref, weight_ref, send_ref, sems):
    width = table_in.shape[1]
    size = weight_ref.shape[1]
    half = width // 2
    first = lax.rem(lax.axis_index("z"), width // size) * size
    into = [
        pltpu.make_async_copy(
            weight_in.at[:, pl.ds(pl.multiple_of(first, size), size)], weight_ref, sems.at[0]
        ),
        pltpu.make_async_copy(table_in, table_ref, sems.at[1]),
    ]
    for copy in into:
        copy.start()
    for copy in into:
        copy.wait()
    weight = weight_ref[...]
    table = table_ref[...].astype(F32)
    left, right = table[:, :half], table[:, half:]
    narrow = jnp.concatenate([left[:8], right[:8], left[8:], right[8:]], 0).astype(BF)
    for tile in range(send_ref.shape[0] // 32):
        send_ref[tile * 32 : (tile + 1) * 32, :size] = weight
        send_ref[tile * 32 : (tile + 1) * 32, size:] = narrow
    back = pltpu.make_async_copy(send_ref, out_ref, sems.at[2])
    back.start()
    back.wait()


def shared_blocks(table, weight, members):
    width = table.shape[1]
    size = width // PLANES
    shape = (members * 16, size + width // 2)
    return pl.pallas_call(
        shared_kernel,
        in_specs=hbm(2),
        out_specs=hbm(1)[0],
        out_shape=pltpu.HBM(shape, BF),
        scratch_shapes=[
            pltpu.VMEM(table.shape, BF),
            pltpu.VMEM((weight.shape[0], size), BF),
            pltpu.VMEM(shape, BF),
            pltpu.SemaphoreType.DMA((3,)),
        ],
        compiler_params=pltpu.CompilerParams(**PARAMS),
        cost_estimate=estimate(2 * shape[0] * shape[1], 2 * shape[0] * shape[1]),
        name="shared_blocks",
    )(*in_hbm(table, weight))


def weight_copies(near_in, far_in, weight_ref, sems):
    width = weight_ref.shape[3]
    size = width // PLANES
    z, core = lax.axis_index("z"), lax.axis_index("c")
    copies = []
    for source, side in ((near_in, core), (far_in, 1 - core)):
        for n, shift in enumerate(SHIFTS):
            first = pl.multiple_of(lax.rem(z + shift + PLANES, PLANES) * size, size)
            copies.append(
                pltpu.make_async_copy(
                    source.at[:, :, n * size : (n + 1) * size],
                    weight_ref.at[:, side, :, pl.ds(first, size)],
                    sems.at[len(copies)],
                )
            )
    return copies


def causal_mask(segment_row):
    n = segment_row.shape[1]
    spread = jnp.broadcast_to(segment_row.astype(F32), (n, n))
    rows = lax.broadcasted_iota(jnp.int32, (n, n), 0)
    cols = lax.broadcasted_iota(jnp.int32, (n, n), 1)
    return (spread == spread.T) & (cols <= rows)


def in_pieces(value):
    high = value.astype(BF).astype(F32)
    middle = (value - high).astype(BF).astype(F32)
    return high, middle, value - high - middle


def forward_kernel(
    order_ref, segments_ref, got_ref, near_in, far_in, negatives_ref, targets_ref, ratios_ref,
    topk_ref,
    invd_ref, inv_ref, pair_out, sums_out, user_out, item_out, pre_out, normed_out,
    pre_ref, normed_ref, resid_ref, pair_ref, sums_ref, user_ref, item_ref, weight_ref, near_ref,
    far_ref, in_sems, out_sems,
):
    slots = got_ref.shape[0]
    rows, width = normed_ref.shape
    items = item_ref.shape[0]
    head = width // HEADS
    half = width // 2
    into = weight_copies(near_in, far_in, weight_ref, in_sems)
    into += [
        pltpu.make_async_copy(near_in.at[:, :, width:], near_ref, in_sems.at[2 * PLANES]),
        pltpu.make_async_copy(far_in.at[:, :, width:], far_ref, in_sems.at[2 * PLANES + 1]),
    ]
    for copy in into:
        copy.start()
    ids = lax.broadcasted_iota(jnp.int32, (slots, rows), 0)
    pick = (ids == order_ref[...]).astype(F32).T.astype(BF)
    for part in range(4):
        columns = slice(part * width, (part + 1) * width)
        pre_ref[:, columns] = dot_nn(pick, got_ref[:, columns]).astype(BF)
    resid_ref[...] = dot_nn(pick, got_ref[:, 4 * width :])
    save_pre = pltpu.make_async_copy(pre_ref, pre_out, out_sems.at[2])
    save_pre.start()
    mask = causal_mask(segments_ref[...])
    scaling = head ** (-0.5)

    def activated(part, h):
        start = part * width + h * head
        values = pre_ref[:, start : start + head].astype(F32)
        return values * sigmoid(values)

    for h in range(HEADS):
        value_h = activated(1, h).astype(BF)
        query_h = activated(2, h).astype(BF)
        key_h = activated(3, h).astype(BF)
        scores = dot_nt(query_h, key_h) * scaling
        att = jnp.where(mask, scores * sigmoid(scores), 0.0) * (2.0 / rows)
        normed_ref[:, h * head : (h + 1) * head] = dot_nn(att.astype(BF), value_h)
    mixed = normed_ref[...]
    centered = mixed - jnp.mean(mixed, 1, keepdims=True)
    inv_dev = lax.rsqrt(jnp.mean(centered * centered, 1, keepdims=True) + 1e-05)
    normed = centered * inv_dev
    normed_ref[...] = normed
    save_normed = pltpu.make_async_copy(normed_ref, normed_out, out_sems.at[3])
    save_normed.start()
    invd_ref[...] = inv_dev
    gate = pre_ref[:, :width].astype(F32)
    gated = (normed * (gate * sigmoid(gate))).astype(BF)
    for copy in into:
        copy.wait()
    weight = weight_ref[...].reshape(width, width)
    output = resid_ref[...] + dot_nn(gated, weight)
    inverse = lax.rsqrt(jnp.sum(output * output, 1, keepdims=True) + 1e-06)
    user = output * inverse
    user_ref[...] = user
    save_user = pltpu.make_async_copy(user_ref, user_out, out_sems.at[0])
    save_user.start()
    inv_ref[...] = inverse
    user_bf = user.astype(BF)
    drawn = negatives_ref.shape[1]
    hits = (lax.broadcasted_iota(jnp.int32, (items, drawn), 0) == negatives_ref[...]).astype(F32)
    counts = dot_nt(jnp.ones((8, drawn), BF), hits.astype(BF))[:1]
    ids = lax.broadcasted_iota(jnp.int32, (rows, items), 1)
    target = as_column(targets_ref[...].astype(F32)).astype(jnp.int32)
    onehot = jnp.where(ids == target, 1.0, 0.0)
    first = lax.axis_index("c") == 0
    near = near_ref[...].astype(F32)
    far = far_ref[...].astype(F32)
    near = jnp.concatenate([near[:, :8], near[:, 8:]], 2)
    far = jnp.concatenate([far[:, :8], far[:, 8:]], 2)
    low = jnp.where(first, near, far)
    high = jnp.where(first, far, near)
    values = jnp.concatenate([low, high], 1).reshape(items, width)
    item_inv = lax.rsqrt(jnp.sum(values * values, 1, keepdims=True) + 1e-06)
    item_ref[...] = (values * item_inv).astype(BF)
    save_item = pltpu.make_async_copy(item_ref, item_out, out_sems.at[1])
    save_item.start()
    logits = SHARP * dot_nt(user_bf, item_ref[...])
    mass = (counts + onehot) * jnp.exp(logits)
    totals = jnp.sum(mass, 1, keepdims=True)
    positive = jnp.sum(onehot * logits, 1, keepdims=True)
    rest = 1.0 - jnp.exp(positive) / totals
    row_loss = jnp.log(totals) - positive
    size = topk_ref[0]
    power = jnp.ones_like(rest)
    square = rest
    for bit in range(4):
        power = jnp.where((((size - 1) >> bit) & 1) == 1, power * square, power)
        square = square * square
    ratio = as_column(ratios_ref[...])
    row_weight = ratio * (size.astype(F32) * power)
    grad = (SHARP * row_weight) * (mass / totals - onehot)
    pair_ref[:, :items] = grad.astype(BF)
    pair_ref[:, items:] = user_bf
    save_pair = pltpu.make_async_copy(pair_ref, pair_out, out_sems.at[5])
    save_pair.start()
    numerator = jnp.sum(row_weight * row_loss, 0, keepdims=True)
    lanes = lax.broadcasted_iota(jnp.int32, sums_ref.shape[1:], 1)
    both = jnp.where(lanes == 0, numerator, jnp.sum(ratio, 0, keepdims=True))
    sums_ref[...] = jnp.broadcast_to(both[None], sums_ref.shape)
    save_sums = pltpu.make_async_copy(sums_ref, sums_out, out_sems.at[4])
    save_sums.start()
    for copy in [save_user, save_item, save_pre, save_normed, save_sums, save_pair]:
        copy.wait()


def forward_pass(order, segments, got, near, far, negatives, targets, ratios, topk, copies):
    rows = order.shape[1]
    width = got.shape[1] // 5
    members, block = near.shape[:2]
    items = members * block
    return pl.pallas_call(
        forward_kernel,
        in_specs=vmem(3) + hbm(2) + vmem(3) + [pl.BlockSpec(memory_space=pltpu.SMEM)],
        out_specs=vmem(2) + hbm(6),
        out_shape=[
            jax.ShapeDtypeStruct((rows, 1), F32),
            jax.ShapeDtypeStruct((rows, 1), F32),
            pltpu.HBM((rows, items + width), BF),
            pltpu.HBM((copies, 8, 128), F32),
            pltpu.HBM((rows, width), F32),
            pltpu.HBM((items, width), BF),
            pltpu.HBM((rows, 4 * width), BF),
            pltpu.HBM((rows, width), F32),
        ],
        scratch_shapes=[
            pltpu.VMEM((rows, 4 * width), BF),
            pltpu.VMEM((rows, width), F32),
            pltpu.VMEM((rows, width), F32),
            pltpu.VMEM((rows, items + width), BF),
            pltpu.VMEM((copies, 8, 128), F32),
            pltpu.VMEM((rows, width), F32),
            pltpu.VMEM((items, width), BF),
            pltpu.VMEM((members, 2, block, width), BF),
            pltpu.VMEM((members, block, width // 2), BF),
            pltpu.VMEM((members, block, width // 2), BF),
            pltpu.SemaphoreType.DMA((2 * PLANES + 2,)),
            pltpu.SemaphoreType.DMA((6,)),
        ],
        compiler_params=pltpu.CompilerParams(**PARAMS),
        cost_estimate=estimate(2 * rows * width * 2816, 12 * 1024 * 1024),
        name="forward_pass",
    )(order, segments, got, *in_hbm(near, far), negatives, targets, ratios, topk)


def items_kernel(own_in, other_ref, out_ref, own_ref, ditem_ref, in_sem, out_sem):
    load = pltpu.make_async_copy(own_in, own_ref, in_sem)
    load.start()
    chips, _, block, width = ditem_ref.shape
    items = chips * 2 * block
    core = lax.axis_index("c")
    load.wait()
    users = jnp.concatenate([own_ref[:, items:], other_ref[:, items:]], 0)
    grads = jnp.concatenate([own_ref[:, :items], other_ref[:, :items]], 0)
    steps = 4
    part = chips // steps
    for step in range(steps):
        at = slice(step * part, (step + 1) * part)
        some = grads[:, step * items // steps : (step + 1) * items // steps]
        ditem_ref[at] = dot_tn(some, users).astype(BF).reshape(part, 2, block, width)
    back = pltpu.make_async_copy(ditem_ref.at[:, core], out_ref, out_sem)
    back.start()
    back.wait()


def items_pass(own, other, chips, items):
    rows, columns = own.shape
    width = columns - items
    block = items // (2 * chips)
    return pl.pallas_call(
        items_kernel,
        in_specs=hbm(1) + vmem(1),
        out_specs=vmem(1)[0],
        out_shape=jax.ShapeDtypeStruct((chips, block, width), BF),
        scratch_shapes=[
            pltpu.VMEM((rows, columns), BF),
            pltpu.VMEM((chips, 2, block, width), BF),
            pltpu.SemaphoreType.DMA,
            pltpu.SemaphoreType.DMA,
        ],
        compiler_params=pltpu.CompilerParams(**PARAMS),
        cost_estimate=estimate(4 * rows * items * width, 4 * 1024 * 1024),
        name="items_pass",
    )(*in_hbm(own), other)


def join_kernel(ditem_ref, sums_ref, inv_ref, out_ref, same_ref, extra_ref, sems):
    chips, block, width = ditem_ref.shape
    first = pltpu.make_async_copy(ditem_ref, out_ref.at[:, :, :width], sems.at[0])
    first.start()
    same_ref[...] = inv_ref[...]
    row = jnp.sum(sums_ref[...], 0)[:1]
    lanes = lax.broadcasted_iota(jnp.int32, row.shape, 1)
    numerator = jnp.sum(jnp.where(lanes == 0, row, 0.0), 1, keepdims=True)
    total = jnp.sum(jnp.where(lanes == 1, row, 0.0), 1, keepdims=True)
    places = lax.broadcasted_iota(jnp.int32, (block, 128), 1)
    extra = jnp.zeros((block, 128), F32)
    for lane, piece in enumerate(in_pieces(numerator) + in_pieces(total)):
        extra = jnp.where(places == lane, piece, extra)
    extra_ref[...] = jnp.broadcast_to(extra.astype(BF)[None], extra_ref.shape)
    second = pltpu.make_async_copy(extra_ref, out_ref.at[:, :, width:], sems.at[1])
    second.start()
    first.wait()
    second.wait()


def join(d_item, sums, inv):
    chips, block, width = d_item.shape
    return pl.pallas_call(
        join_kernel,
        in_specs=vmem(3),
        out_specs=hbm(1) + vmem(1),
        out_shape=[
            pltpu.HBM((chips, block, width + 128), BF),
            jax.ShapeDtypeStruct(inv.shape, F32),
        ],
        scratch_shapes=[
            pltpu.VMEM((chips, block, 128), BF),
            pltpu.SemaphoreType.DMA((2,)),
        ],
        compiler_params=pltpu.CompilerParams(**PARAMS),
        cost_estimate=estimate(d_item.size, 4 * d_item.size),
        name="join",
    )(d_item, sums, inv)


def back_kernel(
    invd_ref, segments_ref, invo_ref, pair_in, item_in, user_in, near_in, far_in, normed_in, pre_in,
    out_ref,
    grad_ref, item_ref, user_ref, weight_ref, normed_ref, pre_ref, sems, weight_sems,
):
    rows, width = normed_ref.shape
    items = item_ref.shape[0]
    head = width // HEADS
    loads = [
        (pair_in.at[:, :items], grad_ref), (item_in, item_ref), (user_in, user_ref),
        (normed_in, normed_ref), (pre_in, pre_ref),
    ]
    loads = [pltpu.make_async_copy(p, q, sems.at[n]) for n, (p, q) in enumerate(loads)]
    into = weight_copies(near_in, far_in, weight_ref, weight_sems)
    for copy in loads[:3] + into + loads[3:]:
        copy.start()
    mask = causal_mask(segments_ref[...])
    for copy in loads[:3]:
        copy.wait()
    user = user_ref[...]
    d_user = dot_nn(grad_ref[...], item_ref[...])
    d_output = invo_ref[...] * (d_user - user * jnp.sum(user * d_user, 1, keepdims=True))
    for copy in into:
        copy.wait()
    d_gated = dot_nt(d_output.astype(BF), weight_ref[...].reshape(width, width))
    loads[3].wait()
    loads[4].wait()
    normed = normed_ref[...]
    gate = pre_ref[:, :width].astype(F32)
    gate_s = sigmoid(gate)
    d_normed = d_gated * (gate * gate_s)
    d_gate = d_gated * normed
    out_ref[:, :width] = d_gate * (gate_s * (1.0 + gate * (1.0 - gate_s)))
    d_mixed = invd_ref[...] * (
        d_normed
        - jnp.mean(d_normed, 1, keepdims=True)
        - normed * jnp.mean(d_normed * normed, 1, keepdims=True)
    )
    dmix_bf = d_mixed.astype(BF)
    scaling = head ** (-0.5)

    def opened(part, h):
        start = part * width + h * head
        values = pre_ref[:, start : start + head].astype(F32)
        logistic = sigmoid(values)
        slope = logistic * (1.0 + values * (1.0 - logistic))
        return (values * logistic).astype(BF), slope

    for h in range(HEADS):
        value_h, value_slope = opened(1, h)
        query_h, query_slope = opened(2, h)
        key_h, key_slope = opened(3, h)
        scores = dot_nt(query_h, key_h) * scaling
        logistic = sigmoid(scores)
        att = jnp.where(mask, scores * logistic, 0.0) * (2.0 / rows)
        dmix_h = dmix_bf[:, h * head : (h + 1) * head]
        d_att = dot_nt(dmix_h, value_h)
        d_value = dot_tn(att.astype(BF), dmix_h)
        slope = logistic * (1.0 + scores * (1.0 - logistic))
        d_scores = jnp.where(mask, d_att * slope, 0.0) * (scaling * 2.0 / rows)
        d_scores = d_scores.astype(BF)
        d_query = dot_nn(d_scores, key_h)
        d_key = dot_tn(d_scores, query_h)
        for part, grad, rate in (
            (1, d_value, value_slope), (2, d_query, query_slope), (3, d_key, key_slope)
        ):
            start = part * width + h * head
            out_ref[:, start : start + head] = grad * rate


def back_pass(inv_dev, segments, inv_out, pair, item, user, near, far, normed, pre):
    rows, width = normed.shape
    items = item.shape[0]
    members, block = near.shape[:2]
    return pl.pallas_call(
        back_kernel,
        in_specs=vmem(3) + hbm(7),
        out_specs=vmem(1)[0],
        out_shape=jax.ShapeDtypeStruct((rows, 4 * width), F32),
        scratch_shapes=[
            pltpu.VMEM((rows, items), BF),
            pltpu.VMEM((items, width), BF),
            pltpu.VMEM((rows, width), F32),
            pltpu.VMEM((members, 2, block, width), BF),
            pltpu.VMEM((rows, width), F32),
            pltpu.VMEM((rows, 4 * width), BF),
            pltpu.SemaphoreType.DMA((5,)),
            pltpu.SemaphoreType.DMA((2 * PLANES,)),
        ],
        compiler_params=pltpu.CompilerParams(**PARAMS),
        cost_estimate=estimate(2 * rows * width * 2304, 8 * 1024 * 1024),
        name="back_pass",
    )(inv_dev, segments, inv_out, *in_hbm(pair, item, user, near, far, normed, pre))


def finish_kernel(
    got_ref, table_ref, act_ref, loss_ref, proj_out, table_out, proj_ref, dtable_ref, sems
):
    width = table_ref.shape[1]
    row = jnp.sum(got_ref[:, :, width:].astype(F32), 0)[:1]
    lanes = lax.broadcasted_iota(jnp.int32, row.shape, 1)
    numerator = jnp.sum(jnp.where(lanes < 3, row, 0.0), 1, keepdims=True)
    total = jnp.sum(jnp.where(lanes < 3, 0.0, row), 1, keepdims=True)
    share = 1.0 / total
    steps = sems.shape[0] - 1
    size = act_ref.shape[0] // steps
    out = []
    for step in range(steps):
        at = slice(step * size, (step + 1) * size)
        proj_ref[at, :] = (act_ref[at, :] * share).astype(BF)
        out.append(pltpu.make_async_copy(proj_ref.at[at, :], proj_out.at[at, :], sems.at[step]))
        out[-1].start()
    loss_ref[...] = jnp.broadcast_to(numerator * share, loss_ref.shape)
    summed = jnp.sum(got_ref[:, :, :width].astype(F32), 0)
    own = table_ref[...].astype(F32)
    inverse = lax.rsqrt(jnp.sum(own * own, 1, keepdims=True) + 1e-06)
    item = own * inverse
    inner = jnp.sum(item * summed, 1, keepdims=True)
    dtable_ref[...] = (share * inverse) * (summed - item * inner)
    out.append(pltpu.make_async_copy(dtable_ref, table_out, sems.at[steps]))
    out[-1].start()
    for copy in out:
        copy.wait()


def finish(got, table, d_act):
    rows, columns = d_act.shape
    return pl.pallas_call(
        finish_kernel,
        in_specs=vmem(3),
        out_specs=vmem(1) + hbm(2),
        out_shape=[
            jax.ShapeDtypeStruct((1, 128), F32),
            pltpu.HBM((rows, columns), BF),
            pltpu.HBM(table.shape, F32),
        ],
        scratch_shapes=[
            pltpu.VMEM((rows, columns), BF),
            pltpu.VMEM(table.shape, F32),
            pltpu.SemaphoreType.DMA((5,)),
        ],
        compiler_params=pltpu.CompilerParams(**PARAMS),
        cost_estimate=estimate(rows * columns, rows * columns * 6),
        name="finish",
    )(got, table, d_act)


def shards(
    proj, resid, send_rows, pack_rows, segments, targets, ratios, negatives, table, out_weight, topk,
    *, groups, members,
):
    width = resid.shape[1]
    mine = table.shape[0]
    with jax.named_scope("shared"):
        share = shared_blocks(table, out_weight, members)
        share = lax.all_to_all(
            share.reshape(members, mine, share.shape[1]), MEMBERS, 0, 0, tiled=True
        )
    with jax.named_scope("route"):
        send = send_blocks(send_rows, proj, resid)
        got = lax.all_to_all(
            send.reshape(members, -1, 5 * width), MEMBERS, 0, 0, tiled=True
        ).reshape(send.shape)
    with jax.named_scope("planes"):
        size = width // PLANES
        mine_part = share[:, :, :size]
        parts = [mine_part]
        for shift in SHIFTS[1:]:
            pairs = [(i, (i - shift) % groups) for i in range(groups)]
            parts.append(lax.ppermute(mine_part, "z", pairs))
        near = jnp.concatenate(parts + [share[:, :, size:]], 2)
        far = lax.ppermute(near, "c", [(0, 1), (1, 0)])
    inv_dev, inv_out, pair, sums, user, item, pre, normed = forward_pass(
        pack_rows, segments, got, near, far, negatives, targets, ratios, topk, 2 * groups
    )
    with jax.named_scope("sums"):
        sums = lax.all_to_all(sums, ("z", "c"), 0, 0, tiled=True)
    with jax.named_scope("items_back"):
        pair_other = lax.ppermute(pair, "c", [(0, 1), (1, 0)])
        d_item = items_pass(pair, pair_other, members // 2, members * mine)
        d_item, inv_out = join(d_item, sums, inv_out)
        got_item = lax.all_to_all(d_item, ("x", "y"), 0, 0, tiled=True)
    d_act = back_pass(inv_dev, segments, inv_out, pair, item, user, near, far, normed, pre)
    loss, d_proj, d_table = finish(got_item, table, d_act)
    return (loss[0, :1], d_proj, d_table)


def solution(mesh):
    groups, members = mesh.devices.shape
    side = 4
    fine = Mesh(
        mesh.devices.reshape(groups, side, members // (2 * side), 2), ("z", "x", "y", "c")
    )

    def body(*args):
        return shards(*args, groups=groups, members=members)

    return jax.shard_map(
        body,
        mesh=fine,
        in_specs=(
            P(EVERY, None),
            P(EVERY, None),
            P(EVERY, None),
            P(EVERY, None),
            P(EVERY, None),
            P(EVERY, None),
            P(EVERY, None),
            P("z", None),
            P(EVERY, None),
            P(MEMBERS, None),
            P(),
        ),
        out_specs=(P(), P(EVERY, None), P(EVERY, None)),
        check_vma=False,
    )
```

```python
import jax
import jax.numpy as jnp
from jax import lax
from jax.experimental import pallas as pl
from jax.experimental.pallas import tpu as pltpu
from jax.sharding import Mesh, PartitionSpec as P

HEADS = 8
SHARP = 20.0
BF = jnp.bfloat16
F32 = jnp.float32
MEMBERS = ("x", "y", "c")
EVERY = ("z", "x", "y", "c")
PLANES = 4
SHIFTS = (0, 1, -1, 2)
PARAMS = dict(vmem_limit_bytes=32 * 1024 * 1024)


def dot_nn(a, b):
    return lax.dot_general(a, b, (((1,), (0,)), ((), ())), preferred_element_type=F32)


def dot_nt(a, b):
    return lax.dot_general(a, b, (((1,), (1,)), ((), ())), preferred_element_type=F32)


def dot_tn(a, b):
    return lax.dot_general(a, b, (((0,), (0,)), ((), ())), preferred_element_type=F32)


def sigmoid(values):
    return 1.0 / (1.0 + jnp.exp(-values))


def vmem(count):
    return [pl.BlockSpec(memory_space=pltpu.VMEM)] * count


def estimate(flops, nbytes, trans=0):
    return pl.CostEstimate(flops=flops, bytes_accessed=nbytes, transcendentals=trans)


def hbm(count):
    return [pl.BlockSpec(memory_space=pltpu.HBM)] * count


def in_hbm(*arrays):
    return [pltpu.with_memory_space_constraint(a, pltpu.HBM) for a in arrays]


def send_kernel(slots_in, proj_in, resid_in, out_ref, slots_ref, rows_ref, send_ref, in_sems, out_sems):
    rows, width = resid_in.shape
    slots = slots_ref.shape[1]
    parts = [slice(n * width, (n + 1) * width) for n in range(5)]
    first = pltpu.make_async_copy(slots_in, slots_ref, in_sems.at[5])
    first.start()
    into = []
    for n, part in enumerate(parts):
        source = resid_in if n == 4 else proj_in.at[:, part]
        into.append(pltpu.make_async_copy(source, rows_ref.at[:, part], in_sems.at[n]))
        into[-1].start()
    first.wait()
    ids = lax.broadcasted_iota(jnp.int32, (rows, slots), 0)
    pick = (ids == slots_ref[...]).astype(F32).T.astype(BF)
    out = []
    for n, part in enumerate(parts):
        into[n].wait()
        send_ref[:, part] = dot_nn(pick, rows_ref[:, part]).astype(BF)
        out.append(pltpu.make_async_copy(send_ref.at[:, part], out_ref.at[:, part], out_sems.at[n]))
        out[-1].start()
    for copy in out:
        copy.wait()


def send_blocks(slots, proj, resid):
    rows, width = resid.shape
    count = slots.shape[1]
    return pl.pallas_call(
        send_kernel,
        in_specs=hbm(3),
        out_specs=hbm(1)[0],
        out_shape=pltpu.HBM((count, 5 * width), BF),
        scratch_shapes=[
            pltpu.VMEM((1, count), jnp.int32),
            pltpu.VMEM((rows, 5 * width), BF),
            pltpu.VMEM((count, 5 * width), BF),
            pltpu.SemaphoreType.DMA((6,)),
            pltpu.SemaphoreType.DMA((5,)),
        ],
        compiler_params=pltpu.CompilerParams(**PARAMS),
        cost_estimate=estimate(2 * count * rows * 5 * width, 2 * 5 * width * (rows + count)),
        name="send_blocks",
    )(*in_hbm(slots, proj, resid))


def shared_kernel(table_in, weight_in, out_ref, table_ref, weight_ref, send_ref, sems):
    width = table_in.shape[1]
    size = weight_ref.shape[1]
    half = width // 2
    first = lax.rem(lax.axis_index("z"), width // size) * size
    into = [
        pltpu.make_async_copy(
            weight_in.at[:, pl.ds(pl.multiple_of(first, size), size)], weight_ref, sems.at[0]
        ),
        pltpu.make_async_copy(table_in, table_ref, sems.at[1]),
    ]
    for copy in into:
        copy.start()
    for copy in into:
        copy.wait()
    weight = weight_ref[...]
    table = table_ref[...].astype(F32)
    left, right = table[:, :half], table[:, half:]
    narrow = jnp.concatenate([left[:8], right[:8], left[8:], right[8:]], 0).astype(BF)
    for tile in range(send_ref.shape[0] // 32):
        send_ref[tile * 32 : (tile + 1) * 32, :size] = weight
        send_ref[tile * 32 : (tile + 1) * 32, size:] = narrow
    back = pltpu.make_async_copy(send_ref, out_ref, sems.at[2])
    back.start()
    back.wait()


def shared_blocks(table, weight, members):
    width = table.shape[1]
    size = width // PLANES
    shape = (members * 16, size + width // 2)
    return pl.pallas_call(
        shared_kernel,
        in_specs=hbm(2),
        out_specs=hbm(1)[0],
        out_shape=pltpu.HBM(shape, BF),
        scratch_shapes=[
            pltpu.VMEM(table.shape, BF),
            pltpu.VMEM((weight.shape[0], size), BF),
            pltpu.VMEM(shape, BF),
            pltpu.SemaphoreType.DMA((3,)),
        ],
        compiler_params=pltpu.CompilerParams(**PARAMS),
        cost_estimate=estimate(2 * shape[0] * shape[1], 2 * shape[0] * shape[1]),
        name="shared_blocks",
    )(*in_hbm(table, weight))


def weight_copies(near_in, far_in, weight_ref, sems):
    width = weight_ref.shape[3]
    size = width // PLANES
    z, core = lax.axis_index("z"), lax.axis_index("c")
    copies = []
    for source, side in ((near_in, core), (far_in, 1 - core)):
        for n, shift in enumerate(SHIFTS):
            first = pl.multiple_of(lax.rem(z + shift + PLANES, PLANES) * size, size)
            copies.append(
                pltpu.make_async_copy(
                    source.at[:, :, n * size : (n + 1) * size],
                    weight_ref.at[:, side, :, pl.ds(first, size)],
                    sems.at[len(copies)],
                )
            )
    return copies


def causal_mask(segment_row):
    n = segment_row.shape[1]
    spread = jnp.broadcast_to(segment_row.astype(F32), (n, n))
    rows = lax.broadcasted_iota(jnp.int32, (n, n), 0)
    cols = lax.broadcasted_iota(jnp.int32, (n, n), 1)
    return (spread == spread.T) & (cols <= rows)


def in_pieces(value):
    high = value.astype(BF).astype(F32)
    middle = (value - high).astype(BF).astype(F32)
    return high, middle, value - high - middle


def unit_items(near_ref, far_ref, items):
    first = lax.axis_index("c") == 0
    near = near_ref[...].astype(F32)
    far = far_ref[...].astype(F32)
    near = jnp.concatenate([near[:, :8], near[:, 8:]], 2)
    far = jnp.concatenate([far[:, :8], far[:, 8:]], 2)
    low = jnp.where(first, near, far)
    high = jnp.where(first, far, near)
    values = jnp.concatenate([low, high], 1).reshape(items, near.shape[2])
    inverse = lax.rsqrt(jnp.sum(values * values, 1, keepdims=True) + 1e-06)
    return (values * inverse).astype(BF)


def forward_kernel(
    order_ref, segments_ref, got_ref, near_in, far_in, negatives_ref, targets_ref, ratios_ref,
    topk_ref,
    invd_ref, inv_ref, pair_out, sums_out, user_out, pre_out, normed_out,
    pre_ref, normed_ref, resid_ref, pair_ref, sums_ref, user_ref, item_ref, weight_ref, near_ref,
    far_ref, in_sems, out_sems,
):
    slots = got_ref.shape[0]
    rows, width = normed_ref.shape
    items = item_ref.shape[0]
    head = width // HEADS
    half = width // 2
    into = weight_copies(near_in, far_in, weight_ref, in_sems)
    into += [
        pltpu.make_async_copy(near_in.at[:, :, width:], near_ref, in_sems.at[2 * PLANES]),
        pltpu.make_async_copy(far_in.at[:, :, width:], far_ref, in_sems.at[2 * PLANES + 1]),
    ]
    for copy in into:
        copy.start()
    ids = lax.broadcasted_iota(jnp.int32, (slots, rows), 0)
    pick = (ids == order_ref[...]).astype(F32).T.astype(BF)
    for part in range(4):
        columns = slice(part * width, (part + 1) * width)
        pre_ref[:, columns] = dot_nn(pick, got_ref[:, columns]).astype(BF)
    resid_ref[...] = dot_nn(pick, got_ref[:, 4 * width :])
    save_pre = pltpu.make_async_copy(pre_ref, pre_out, out_sems.at[2])
    save_pre.start()
    mask = causal_mask(segments_ref[...])
    scaling = head ** (-0.5)

    def activated(part, h):
        start = part * width + h * head
        values = pre_ref[:, start : start + head].astype(F32)
        return values * sigmoid(values)

    for h in range(HEADS):
        value_h = activated(1, h).astype(BF)
        query_h = activated(2, h).astype(BF)
        key_h = activated(3, h).astype(BF)
        scores = dot_nt(query_h, key_h) * scaling
        att = jnp.where(mask, scores * sigmoid(scores), 0.0) * (2.0 / rows)
        normed_ref[:, h * head : (h + 1) * head] = dot_nn(att.astype(BF), value_h)
    mixed = normed_ref[...]
    centered = mixed - jnp.mean(mixed, 1, keepdims=True)
    inv_dev = lax.rsqrt(jnp.mean(centered * centered, 1, keepdims=True) + 1e-05)
    normed = centered * inv_dev
    normed_ref[...] = normed
    save_normed = pltpu.make_async_copy(normed_ref, normed_out, out_sems.at[3])
    save_normed.start()
    invd_ref[...] = inv_dev
    gate = pre_ref[:, :width].astype(F32)
    gated = (normed * (gate * sigmoid(gate))).astype(BF)
    for copy in into:
        copy.wait()
    weight = weight_ref[...].reshape(width, width)
    output = resid_ref[...] + dot_nn(gated, weight)
    inverse = lax.rsqrt(jnp.sum(output * output, 1, keepdims=True) + 1e-06)
    user = output * inverse
    user_ref[...] = user
    save_user = pltpu.make_async_copy(user_ref, user_out, out_sems.at[0])
    save_user.start()
    inv_ref[...] = inverse
    user_bf = user.astype(BF)
    lane = 128
    for n in range(width // lane):
        pair_ref[items + n * rows : items + (n + 1) * rows, :] = user_bf[:, n * lane : (n + 1) * lane]
    save_half = pltpu.make_async_copy(
        pair_ref.at[items:, :], pair_out.at[items:, :], out_sems.at[1]
    )
    save_half.start()
    item_ref[...] = unit_items(near_ref, far_ref, items)
    drawn = negatives_ref.shape[1]
    hits = (lax.broadcasted_iota(jnp.int32, (items, drawn), 0) == negatives_ref[...]).astype(F32)
    counts = dot_nn(hits.astype(BF), jnp.ones((drawn, rows), BF))
    ids = lax.broadcasted_iota(jnp.int32, (items, rows), 0)
    onehot = jnp.where(ids == targets_ref[...], 1.0, 0.0)
    logits = SHARP * dot_nt(item_ref[...], user_bf)
    mass = (counts + onehot) * jnp.exp(logits)
    totals = jnp.sum(mass, 0, keepdims=True)
    positive = jnp.sum(onehot * logits, 0, keepdims=True)
    rest = 1.0 - jnp.exp(positive) / totals
    row_loss = jnp.log(totals) - positive
    size = topk_ref[0]
    power = jnp.ones_like(rest)
    square = rest
    for bit in range(4):
        power = jnp.where((((size - 1) >> bit) & 1) == 1, power * square, power)
        square = square * square
    ratio = ratios_ref[...]
    row_weight = ratio * (size.astype(F32) * power)
    grad = mass * ((SHARP * row_weight) / totals) - onehot * (SHARP * row_weight)
    pair_ref[:items, :] = grad.astype(BF)
    save_pair = pltpu.make_async_copy(
        pair_ref.at[:items, :], pair_out.at[:items, :], out_sems.at[5]
    )
    save_pair.start()
    numerator = jnp.sum(row_weight * row_loss, 1, keepdims=True)
    lanes = lax.broadcasted_iota(jnp.int32, sums_ref.shape[1:], 1)
    both = jnp.where(lanes == 0, numerator, jnp.sum(ratio, 1, keepdims=True))
    sums_ref[...] = jnp.broadcast_to(both[None], sums_ref.shape)
    save_sums = pltpu.make_async_copy(sums_ref, sums_out, out_sems.at[4])
    save_sums.start()
    for copy in [save_user, save_half, save_pre, save_normed, save_sums, save_pair]:
        copy.wait()


def forward_pass(order, segments, got, near, far, negatives, targets, ratios, topk, copies):
    rows = order.shape[1]
    width = got.shape[1] // 5
    members, block = near.shape[:2]
    items = members * block
    return pl.pallas_call(
        forward_kernel,
        in_specs=vmem(3) + hbm(2) + vmem(3) + [pl.BlockSpec(memory_space=pltpu.SMEM)],
        out_specs=vmem(2) + hbm(5),
        out_shape=[
            jax.ShapeDtypeStruct((rows, 1), F32),
            jax.ShapeDtypeStruct((rows, 1), F32),
            pltpu.HBM((items + width // 128 * rows, 128), BF),
            pltpu.HBM((copies, 8, 128), F32),
            pltpu.HBM((rows, width), F32),
            pltpu.HBM((rows, 4 * width), BF),
            pltpu.HBM((rows, width), F32),
        ],
        scratch_shapes=[
            pltpu.VMEM((rows, 4 * width), BF),
            pltpu.VMEM((rows, width), F32),
            pltpu.VMEM((rows, width), F32),
            pltpu.VMEM((items + width // 128 * rows, 128), BF),
            pltpu.VMEM((copies, 8, 128), F32),
            pltpu.VMEM((rows, width), F32),
            pltpu.VMEM((items, width), BF),
            pltpu.VMEM((members, 2, block, width), BF),
            pltpu.VMEM((members, block, width // 2), BF),
            pltpu.VMEM((members, block, width // 2), BF),
            pltpu.SemaphoreType.DMA((2 * PLANES + 2,)),
            pltpu.SemaphoreType.DMA((6,)),
        ],
        compiler_params=pltpu.CompilerParams(**PARAMS),
        cost_estimate=estimate(2 * rows * width * 2816, 12 * 1024 * 1024),
        name="forward_pass",
    )(order, segments, got, *in_hbm(near, far), negatives, targets, ratios, topk)


def items_kernel(own_in, other_ref, out_ref, own_ref, ditem_ref, in_sem, out_sem):
    load = pltpu.make_async_copy(own_in, own_ref, in_sem)
    load.start()
    chips, _, block, width = ditem_ref.shape
    items = chips * 2 * block
    lane = own_ref.shape[1]
    rows = (own_ref.shape[0] - items) * lane // width
    core = lax.axis_index("c")
    load.wait()
    users = []
    for source in (own_ref, other_ref):
        parts = [
            source[items + n * rows : items + (n + 1) * rows, :] for n in range(width // lane)
        ]
        users.append(jnp.concatenate(parts, 1))
    users = jnp.concatenate(users, 0)
    grads = jnp.concatenate([own_ref[:items, :], other_ref[:items, :]], 1)
    steps = 4
    part = chips // steps
    for step in range(steps):
        at = slice(step * part, (step + 1) * part)
        some = grads[step * items // steps : (step + 1) * items // steps]
        ditem_ref[at] = dot_nn(some, users).astype(BF).reshape(part, 2, block, width)
    back = pltpu.make_async_copy(ditem_ref.at[:, core], out_ref, out_sem)
    back.start()
    back.wait()


def items_pass(own, other, chips, items, width):
    block = items // (2 * chips)
    return pl.pallas_call(
        items_kernel,
        in_specs=hbm(1) + vmem(1),
        out_specs=vmem(1)[0],
        out_shape=jax.ShapeDtypeStruct((chips, block, width), BF),
        scratch_shapes=[
            pltpu.VMEM(own.shape, BF),
            pltpu.VMEM((chips, 2, block, width), BF),
            pltpu.SemaphoreType.DMA,
            pltpu.SemaphoreType.DMA,
        ],
        compiler_params=pltpu.CompilerParams(**PARAMS),
        cost_estimate=estimate(512 * items * width, 4 * 1024 * 1024),
        name="items_pass",
    )(*in_hbm(own), other)


def join_kernel(ditem_ref, sums_ref, inv_ref, out_ref, same_ref, extra_ref, sems):
    chips, block, width = ditem_ref.shape
    first = pltpu.make_async_copy(ditem_ref, out_ref.at[:, :, :width], sems.at[0])
    first.start()
    same_ref[...] = inv_ref[...]
    row = jnp.sum(sums_ref[...], 0)[:1]
    lanes = lax.broadcasted_iota(jnp.int32, row.shape, 1)
    numerator = jnp.sum(jnp.where(lanes == 0, row, 0.0), 1, keepdims=True)
    total = jnp.sum(jnp.where(lanes == 1, row, 0.0), 1, keepdims=True)
    places = lax.broadcasted_iota(jnp.int32, (block, 128), 1)
    extra = jnp.zeros((block, 128), F32)
    for lane, piece in enumerate(in_pieces(numerator) + in_pieces(total)):
        extra = jnp.where(places == lane, piece, extra)
    extra_ref[...] = jnp.broadcast_to(extra.astype(BF)[None], extra_ref.shape)
    second = pltpu.make_async_copy(extra_ref, out_ref.at[:, :, width:], sems.at[1])
    second.start()
    first.wait()
    second.wait()


def join(d_item, sums, inv):
    chips, block, width = d_item.shape
    return pl.pallas_call(
        join_kernel,
        in_specs=vmem(3),
        out_specs=hbm(1) + vmem(1),
        out_shape=[
            pltpu.HBM((chips, block, width + 128), BF),
            jax.ShapeDtypeStruct(inv.shape, F32),
        ],
        scratch_shapes=[
            pltpu.VMEM((chips, block, 128), BF),
            pltpu.SemaphoreType.DMA((2,)),
        ],
        compiler_params=pltpu.CompilerParams(**PARAMS),
        cost_estimate=estimate(d_item.size, 4 * d_item.size),
        name="join",
    )(d_item, sums, inv)


def back_kernel(
    invd_ref, segments_ref, invo_ref, pair_in, user_in, near_in, far_in, normed_in, pre_in,
    out_ref,
    grad_ref, near_ref, far_ref, user_ref, weight_ref, normed_ref, pre_ref, sems, weight_sems,
):
    rows, width = normed_ref.shape
    items = grad_ref.shape[0]
    head = width // HEADS
    loads = [
        (pair_in.at[:items, :], grad_ref), (near_in.at[:, :, width:], near_ref),
        (far_in.at[:, :, width:], far_ref), (user_in, user_ref), (normed_in, normed_ref),
        (pre_in, pre_ref),
    ]
    loads = [pltpu.make_async_copy(p, q, sems.at[n]) for n, (p, q) in enumerate(loads)]
    into = weight_copies(near_in, far_in, weight_ref, weight_sems)
    for copy in loads[:4] + into + loads[4:]:
        copy.start()
    mask = causal_mask(segments_ref[...])
    for copy in loads[:4]:
        copy.wait()
    user = user_ref[...]
    d_user = dot_tn(grad_ref[...], unit_items(near_ref, far_ref, items))
    d_output = invo_ref[...] * (d_user - user * jnp.sum(user * d_user, 1, keepdims=True))
    for copy in into:
        copy.wait()
    d_gated = dot_nt(d_output.astype(BF), weight_ref[...].reshape(width, width))
    loads[4].wait()
    loads[5].wait()
    normed = normed_ref[...]
    gate = pre_ref[:, :width].astype(F32)
    gate_s = sigmoid(gate)
    d_normed = d_gated * (gate * gate_s)
    d_gate = d_gated * normed
    out_ref[:, :width] = d_gate * (gate_s * (1.0 + gate * (1.0 - gate_s)))
    d_mixed = invd_ref[...] * (
        d_normed
        - jnp.mean(d_normed, 1, keepdims=True)
        - normed * jnp.mean(d_normed * normed, 1, keepdims=True)
    )
    dmix_bf = d_mixed.astype(BF)
    scaling = head ** (-0.5)

    def opened(part, h):
        start = part * width + h * head
        values = pre_ref[:, start : start + head].astype(F32)
        logistic = sigmoid(values)
        slope = logistic * (1.0 + values * (1.0 - logistic))
        return (values * logistic).astype(BF), slope

    for h in range(HEADS):
        value_h, value_slope = opened(1, h)
        query_h, query_slope = opened(2, h)
        key_h, key_slope = opened(3, h)
        scores = dot_nt(query_h, key_h) * scaling
        logistic = sigmoid(scores)
        att = jnp.where(mask, scores * logistic, 0.0) * (2.0 / rows)
        dmix_h = dmix_bf[:, h * head : (h + 1) * head]
        d_att = dot_nt(dmix_h, value_h)
        d_value = dot_tn(att.astype(BF), dmix_h)
        slope = logistic * (1.0 + scores * (1.0 - logistic))
        d_scores = jnp.where(mask, d_att * slope, 0.0) * (scaling * 2.0 / rows)
        d_scores = d_scores.astype(BF)
        d_query = dot_nn(d_scores, key_h)
        d_key = dot_tn(d_scores, query_h)
        for part, grad, rate in (
            (1, d_value, value_slope), (2, d_query, query_slope), (3, d_key, key_slope)
        ):
            start = part * width + h * head
            out_ref[:, start : start + head] = grad * rate


def back_pass(inv_dev, segments, inv_out, pair, user, near, far, normed, pre):
    rows, width = normed.shape
    members, block = near.shape[:2]
    items = members * block
    return pl.pallas_call(
        back_kernel,
        in_specs=vmem(3) + hbm(6),
        out_specs=vmem(1)[0],
        out_shape=jax.ShapeDtypeStruct((rows, 4 * width), F32),
        scratch_shapes=[
            pltpu.VMEM((items, rows), BF),
            pltpu.VMEM((members, block, width // 2), BF),
            pltpu.VMEM((members, block, width // 2), BF),
            pltpu.VMEM((rows, width), F32),
            pltpu.VMEM((members, 2, block, width), BF),
            pltpu.VMEM((rows, width), F32),
            pltpu.VMEM((rows, 4 * width), BF),
            pltpu.SemaphoreType.DMA((6,)),
            pltpu.SemaphoreType.DMA((2 * PLANES,)),
        ],
        compiler_params=pltpu.CompilerParams(**PARAMS),
        cost_estimate=estimate(2 * rows * width * 2304, 8 * 1024 * 1024),
        name="back_pass",
    )(inv_dev, segments, inv_out, *in_hbm(pair, user, near, far, normed, pre))


def finish_kernel(
    got_ref, table_ref, act_ref, loss_ref, proj_out, table_out, proj_ref, dtable_ref, sems
):
    width = table_ref.shape[1]
    row = jnp.sum(got_ref[:, :, width:].astype(F32), 0)[:1]
    lanes = lax.broadcasted_iota(jnp.int32, row.shape, 1)
    numerator = jnp.sum(jnp.where(lanes < 3, row, 0.0), 1, keepdims=True)
    total = jnp.sum(jnp.where(lanes < 3, 0.0, row), 1, keepdims=True)
    share = 1.0 / total
    steps = sems.shape[0] - 1
    size = act_ref.shape[0] // steps
    out = []
    for step in range(steps):
        at = slice(step * size, (step + 1) * size)
        proj_ref[at, :] = (act_ref[at, :] * share).astype(BF)
        out.append(pltpu.make_async_copy(proj_ref.at[at, :], proj_out.at[at, :], sems.at[step]))
        out[-1].start()
    loss_ref[...] = jnp.broadcast_to(numerator * share, loss_ref.shape)
    summed = jnp.sum(got_ref[:, :, :width].astype(F32), 0)
    own = table_ref[...].astype(F32)
    inverse = lax.rsqrt(jnp.sum(own * own, 1, keepdims=True) + 1e-06)
    item = own * inverse
    inner = jnp.sum(item * summed, 1, keepdims=True)
    dtable_ref[...] = (share * inverse) * (summed - item * inner)
    out.append(pltpu.make_async_copy(dtable_ref, table_out, sems.at[steps]))
    out[-1].start()
    for copy in out:
        copy.wait()


def finish(got, table, d_act):
    rows, columns = d_act.shape
    return pl.pallas_call(
        finish_kernel,
        in_specs=vmem(3),
        out_specs=vmem(1) + hbm(2),
        out_shape=[
            jax.ShapeDtypeStruct((1, 128), F32),
            pltpu.HBM((rows, columns), BF),
            pltpu.HBM(table.shape, F32),
        ],
        scratch_shapes=[
            pltpu.VMEM((rows, columns), BF),
            pltpu.VMEM(table.shape, F32),
            pltpu.SemaphoreType.DMA((5,)),
        ],
        compiler_params=pltpu.CompilerParams(**PARAMS),
        cost_estimate=estimate(rows * columns, rows * columns * 6),
        name="finish",
    )(got, table, d_act)


def shards(
    proj, resid, send_rows, pack_rows, segments, targets, ratios, negatives, table, out_weight, topk,
    *, groups, members,
):
    width = resid.shape[1]
    mine = table.shape[0]
    with jax.named_scope("shared"):
        share = shared_blocks(table, out_weight, members)
        share = lax.all_to_all(
            share.reshape(members, mine, share.shape[1]), MEMBERS, 0, 0, tiled=True
        )
    with jax.named_scope("route"):
        send = send_blocks(send_rows, proj, resid)
        got = lax.all_to_all(
            send.reshape(members, -1, 5 * width), MEMBERS, 0, 0, tiled=True
        ).reshape(send.shape)
    with jax.named_scope("planes"):
        size = width // PLANES
        mine_part = share[:, :, :size]
        parts = [mine_part]
        for shift in SHIFTS[1:]:
            pairs = [(i, (i - shift) % groups) for i in range(groups)]
            parts.append(lax.ppermute(mine_part, "z", pairs))
        near = jnp.concatenate(parts + [share[:, :, size:]], 2)
        far = lax.ppermute(near, "c", [(0, 1), (1, 0)])
    inv_dev, inv_out, pair, sums, user, pre, normed = forward_pass(
        pack_rows, segments, got, near, far, negatives, targets, ratios, topk, 2 * groups
    )
    with jax.named_scope("sums"):
        sums = lax.all_to_all(sums, ("z", "c"), 0, 0, tiled=True)
    with jax.named_scope("items_back"):
        pair_other = lax.ppermute(pair, "c", [(0, 1), (1, 0)])
        d_item = items_pass(pair, pair_other, members // 2, members * mine, width)
        d_item, inv_out = join(d_item, sums, inv_out)
        got_item = lax.all_to_all(d_item, ("x", "y"), 0, 0, tiled=True)
    d_act = back_pass(inv_dev, segments, inv_out, pair, user, near, far, normed, pre)
    loss, d_proj, d_table = finish(got_item, table, d_act)
    return (loss[0, :1], d_proj, d_table)


def solution(mesh):
    groups, members = mesh.devices.shape
    side = 4
    fine = Mesh(
        mesh.devices.reshape(groups, side, members // (2 * side), 2), ("z", "x", "y", "c")
    )

    def body(*args):
        return shards(*args, groups=groups, members=members)

    return jax.shard_map(
        body,
        mesh=fine,
        in_specs=(
            P(EVERY, None),
            P(EVERY, None),
            P(EVERY, None),
            P(EVERY, None),
            P(EVERY, None),
            P(EVERY, None),
            P(EVERY, None),
            P("z", None),
            P(EVERY, None),
            P(MEMBERS, None),
            P(),
        ),
        out_specs=(P(), P(EVERY, None), P(EVERY, None)),
        check_vma=False,
    )
```

```python
import jax
import jax.numpy as jnp
from jax import lax
from jax.experimental import pallas as pl
from jax.experimental.pallas import tpu as pltpu
from jax.sharding import Mesh, PartitionSpec as P

HEADS = 8
SHARP = 20.0
BF = jnp.bfloat16
F32 = jnp.float32
MEMBERS = ("x", "y", "c")
EVERY = ("z", "x", "y", "c")
PLANES = 4
SHIFTS = (0, 1, -1, 2)
PARAMS = dict(vmem_limit_bytes=32 * 1024 * 1024)


def dot_nn(a, b):
    return lax.dot_general(a, b, (((1,), (0,)), ((), ())), preferred_element_type=F32)


def dot_nt(a, b):
    return lax.dot_general(a, b, (((1,), (1,)), ((), ())), preferred_element_type=F32)


def dot_tn(a, b):
    return lax.dot_general(a, b, (((0,), (0,)), ((), ())), preferred_element_type=F32)


def sigmoid(values):
    return 0.5 + 0.5 * jnp.tanh(0.5 * values)


def vmem(count):
    return [pl.BlockSpec(memory_space=pltpu.VMEM)] * count


def estimate(flops, nbytes, trans=0):
    return pl.CostEstimate(flops=flops, bytes_accessed=nbytes, transcendentals=trans)


def hbm(count):
    return [pl.BlockSpec(memory_space=pltpu.HBM)] * count


def in_hbm(*arrays):
    return [pltpu.with_memory_space_constraint(a, pltpu.HBM) for a in arrays]


def send_kernel(slots_in, proj_in, resid_in, out_ref, slots_ref, rows_ref, send_ref, in_sems, out_sems):
    rows, width = resid_in.shape
    slots = slots_ref.shape[1]
    parts = [slice(n * width, (n + 1) * width) for n in range(5)]
    first = pltpu.make_async_copy(slots_in, slots_ref, in_sems.at[5])
    first.start()
    into = []
    for n, part in enumerate(parts):
        source = resid_in if n == 4 else proj_in.at[:, part]
        into.append(pltpu.make_async_copy(source, rows_ref.at[:, part], in_sems.at[n]))
        into[-1].start()
    first.wait()
    ids = lax.broadcasted_iota(jnp.int32, (rows, slots), 0)
    pick = (ids == slots_ref[...]).astype(F32).T.astype(BF)
    out = []
    for n, part in enumerate(parts):
        into[n].wait()
        send_ref[:, part] = dot_nn(pick, rows_ref[:, part]).astype(BF)
        out.append(pltpu.make_async_copy(send_ref.at[:, part], out_ref.at[:, part], out_sems.at[n]))
        out[-1].start()
    for copy in out:
        copy.wait()


def send_blocks(slots, proj, resid):
    rows, width = resid.shape
    count = slots.shape[1]
    return pl.pallas_call(
        send_kernel,
        in_specs=hbm(3),
        out_specs=hbm(1)[0],
        out_shape=pltpu.HBM((count, 5 * width), BF),
        scratch_shapes=[
            pltpu.VMEM((1, count), jnp.int32),
            pltpu.VMEM((rows, 5 * width), BF),
            pltpu.VMEM((count, 5 * width), BF),
            pltpu.SemaphoreType.DMA((6,)),
            pltpu.SemaphoreType.DMA((5,)),
        ],
        compiler_params=pltpu.CompilerParams(**PARAMS),
        cost_estimate=estimate(2 * count * rows * 5 * width, 2 * 5 * width * (rows + count)),
        name="send_blocks",
    )(*in_hbm(slots, proj, resid))


def shared_kernel(table_in, weight_in, out_ref, table_ref, weight_ref, send_ref, sems):
    width = table_in.shape[1]
    size = weight_ref.shape[1]
    half = width // 2
    first = lax.rem(lax.axis_index("z"), width // size) * size
    into = [
        pltpu.make_async_copy(
            weight_in.at[:, pl.ds(pl.multiple_of(first, size), size)], weight_ref, sems.at[0]
        ),
        pltpu.make_async_copy(table_in, table_ref, sems.at[1]),
    ]
    for copy in into:
        copy.start()
    for copy in into:
        copy.wait()
    weight = weight_ref[...]
    table = table_ref[...].astype(F32)
    left, right = table[:, :half], table[:, half:]
    narrow = jnp.concatenate([left[:8], right[:8], left[8:], right[8:]], 0).astype(BF)
    for tile in range(send_ref.shape[0] // 32):
        send_ref[tile * 32 : (tile + 1) * 32, :size] = weight
        send_ref[tile * 32 : (tile + 1) * 32, size:] = narrow
    back = pltpu.make_async_copy(send_ref, out_ref, sems.at[2])
    back.start()
    back.wait()


def shared_blocks(table, weight, members):
    width = table.shape[1]
    size = width // PLANES
    shape = (members * 16, size + width // 2)
    return pl.pallas_call(
        shared_kernel,
        in_specs=hbm(2),
        out_specs=hbm(1)[0],
        out_shape=pltpu.HBM(shape, BF),
        scratch_shapes=[
            pltpu.VMEM(table.shape, BF),
            pltpu.VMEM((weight.shape[0], size), BF),
            pltpu.VMEM(shape, BF),
            pltpu.SemaphoreType.DMA((3,)),
        ],
        compiler_params=pltpu.CompilerParams(**PARAMS),
        cost_estimate=estimate(2 * shape[0] * shape[1], 2 * shape[0] * shape[1]),
        name="shared_blocks",
    )(*in_hbm(table, weight))


def weight_copies(near_in, far_in, weight_ref, sems):
    width = weight_ref.shape[3]
    size = width // PLANES
    z, core = lax.axis_index("z"), lax.axis_index("c")
    copies = []
    for source, side in ((near_in, core), (far_in, 1 - core)):
        for n, shift in enumerate(SHIFTS):
            first = pl.multiple_of(lax.rem(z + shift + PLANES, PLANES) * size, size)
            copies.append(
                pltpu.make_async_copy(
                    source.at[:, :, n * size : (n + 1) * size],
                    weight_ref.at[:, side, :, pl.ds(first, size)],
                    sems.at[len(copies)],
                )
            )
    return copies


def causal_mask(segment_row):
    n = segment_row.shape[1]
    spread = jnp.broadcast_to(segment_row.astype(F32), (n, n))
    rows = lax.broadcasted_iota(jnp.int32, (n, n), 0)
    cols = lax.broadcasted_iota(jnp.int32, (n, n), 1)
    return (spread == spread.T) & (cols <= rows)


def in_pieces(value):
    high = value.astype(BF).astype(F32)
    middle = (value - high).astype(BF).astype(F32)
    return high, middle, value - high - middle


def unit_items(near_ref, far_ref, items):
    first = lax.axis_index("c") == 0
    near = near_ref[...].astype(F32)
    far = far_ref[...].astype(F32)
    near = jnp.concatenate([near[:, :8], near[:, 8:]], 2)
    far = jnp.concatenate([far[:, :8], far[:, 8:]], 2)
    low = jnp.where(first, near, far)
    high = jnp.where(first, far, near)
    values = jnp.concatenate([low, high], 1).reshape(items, near.shape[2])
    inverse = lax.rsqrt(jnp.sum(values * values, 1, keepdims=True) + 1e-06)
    return (values * inverse).astype(BF)


def forward_kernel(
    order_ref, segments_ref, got_ref, near_in, far_in, negatives_ref, targets_ref, ratios_ref,
    topk_ref,
    invd_ref, inv_ref, pair_out, sums_out, user_out, pre_out, normed_out,
    pre_ref, normed_ref, resid_ref, pair_ref, sums_ref, user_ref, item_ref, weight_ref, near_ref,
    far_ref, in_sems, out_sems,
):
    slots = got_ref.shape[0]
    rows, width = normed_ref.shape
    items = item_ref.shape[0]
    head = width // HEADS
    half = width // 2
    into = weight_copies(near_in, far_in, weight_ref, in_sems)
    into += [
        pltpu.make_async_copy(near_in.at[:, :, width:], near_ref, in_sems.at[2 * PLANES]),
        pltpu.make_async_copy(far_in.at[:, :, width:], far_ref, in_sems.at[2 * PLANES + 1]),
    ]
    for copy in into:
        copy.start()
    ids = lax.broadcasted_iota(jnp.int32, (slots, rows), 0)
    pick = (ids == order_ref[...]).astype(F32).T.astype(BF)
    for part in range(4):
        columns = slice(part * width, (part + 1) * width)
        pre_ref[:, columns] = dot_nn(pick, got_ref[:, columns]).astype(BF)
    resid_ref[...] = dot_nn(pick, got_ref[:, 4 * width :])
    save_pre = pltpu.make_async_copy(pre_ref, pre_out, out_sems.at[2])
    save_pre.start()
    mask = causal_mask(segments_ref[...])
    scaling = head ** (-0.5)

    def activated(part, h):
        start = part * width + h * head
        values = pre_ref[:, start : start + head].astype(F32)
        return values * sigmoid(values)

    for h in range(HEADS):
        value_h = activated(1, h).astype(BF)
        query_h = activated(2, h).astype(BF)
        key_h = activated(3, h).astype(BF)
        scores = dot_nt(query_h, key_h) * scaling
        att = jnp.where(mask, scores * sigmoid(scores), 0.0) * (2.0 / rows)
        normed_ref[:, h * head : (h + 1) * head] = dot_nn(att.astype(BF), value_h)
    mixed = normed_ref[...]
    centered = mixed - jnp.mean(mixed, 1, keepdims=True)
    inv_dev = lax.rsqrt(jnp.mean(centered * centered, 1, keepdims=True) + 1e-05)
    normed = centered * inv_dev
    normed_ref[...] = normed
    save_normed = pltpu.make_async_copy(normed_ref, normed_out, out_sems.at[3])
    save_normed.start()
    invd_ref[...] = inv_dev
    gate = pre_ref[:, :width].astype(F32)
    gated = (normed * (gate * sigmoid(gate))).astype(BF)
    for copy in into:
        copy.wait()
    weight = weight_ref[...].reshape(width, width)
    output = resid_ref[...] + dot_nn(gated, weight)
    inverse = lax.rsqrt(jnp.sum(output * output, 1, keepdims=True) + 1e-06)
    user = output * inverse
    user_ref[...] = user
    save_user = pltpu.make_async_copy(user_ref, user_out, out_sems.at[0])
    save_user.start()
    inv_ref[...] = inverse
    user_bf = user.astype(BF)
    lane = 128
    for n in range(width // lane):
        pair_ref[items + n * rows : items + (n + 1) * rows, :] = user_bf[:, n * lane : (n + 1) * lane]
    save_half = pltpu.make_async_copy(
        pair_ref.at[items:, :], pair_out.at[items:, :], out_sems.at[1]
    )
    save_half.start()
    item_ref[...] = unit_items(near_ref, far_ref, items)
    drawn = negatives_ref.shape[1]
    hits = (lax.broadcasted_iota(jnp.int32, (items, drawn), 0) == negatives_ref[...]).astype(F32)
    counts = dot_nn(hits.astype(BF), jnp.ones((drawn, rows), BF))
    ids = lax.broadcasted_iota(jnp.int32, (items, rows), 0)
    onehot = jnp.where(ids == targets_ref[...], 1.0, 0.0)
    logits = SHARP * dot_nt(item_ref[...], user_bf)
    mass = (counts + onehot) * jnp.exp(logits)
    totals = jnp.sum(mass, 0, keepdims=True)
    positive = jnp.sum(onehot * logits, 0, keepdims=True)
    rest = 1.0 - jnp.exp(positive) / totals
    row_loss = jnp.log(totals) - positive
    size = topk_ref[0]
    power = jnp.ones_like(rest)
    square = rest
    for bit in range(4):
        power = jnp.where((((size - 1) >> bit) & 1) == 1, power * square, power)
        square = square * square
    ratio = ratios_ref[...]
    row_weight = ratio * (size.astype(F32) * power)
    grad = mass * ((SHARP * row_weight) / totals) - onehot * (SHARP * row_weight)
    pair_ref[:items, :] = grad.astype(BF)
    save_pair = pltpu.make_async_copy(
        pair_ref.at[:items, :], pair_out.at[:items, :], out_sems.at[5]
    )
    save_pair.start()
    numerator = jnp.sum(row_weight * row_loss, 1, keepdims=True)
    lanes = lax.broadcasted_iota(jnp.int32, sums_ref.shape[1:], 1)
    both = jnp.where(lanes == 0, numerator, jnp.sum(ratio, 1, keepdims=True))
    sums_ref[...] = jnp.broadcast_to(both[None], sums_ref.shape)
    save_sums = pltpu.make_async_copy(sums_ref, sums_out, out_sems.at[4])
    save_sums.start()
    for copy in [save_user, save_half, save_pre, save_normed, save_sums, save_pair]:
        copy.wait()


def forward_pass(order, segments, got, near, far, negatives, targets, ratios, topk, copies):
    rows = order.shape[1]
    width = got.shape[1] // 5
    members, block = near.shape[:2]
    items = members * block
    return pl.pallas_call(
        forward_kernel,
        in_specs=vmem(3) + hbm(2) + vmem(3) + [pl.BlockSpec(memory_space=pltpu.SMEM)],
        out_specs=vmem(2) + hbm(5),
        out_shape=[
            jax.ShapeDtypeStruct((rows, 1), F32),
            jax.ShapeDtypeStruct((rows, 1), F32),
            pltpu.HBM((items + width // 128 * rows, 128), BF),
            pltpu.HBM((copies, 8, 128), F32),
            pltpu.HBM((rows, width), F32),
            pltpu.HBM((rows, 4 * width), BF),
            pltpu.HBM((rows, width), F32),
        ],
        scratch_shapes=[
            pltpu.VMEM((rows, 4 * width), BF),
            pltpu.VMEM((rows, width), F32),
            pltpu.VMEM((rows, width), F32),
            pltpu.VMEM((items + width // 128 * rows, 128), BF),
            pltpu.VMEM((copies, 8, 128), F32),
            pltpu.VMEM((rows, width), F32),
            pltpu.VMEM((items, width), BF),
            pltpu.VMEM((members, 2, block, width), BF),
            pltpu.VMEM((members, block, width // 2), BF),
            pltpu.VMEM((members, block, width // 2), BF),
            pltpu.SemaphoreType.DMA((2 * PLANES + 2,)),
            pltpu.SemaphoreType.DMA((6,)),
        ],
        compiler_params=pltpu.CompilerParams(**PARAMS),
        cost_estimate=estimate(2 * rows * width * 2816, 12 * 1024 * 1024),
        name="forward_pass",
    )(order, segments, got, *in_hbm(near, far), negatives, targets, ratios, topk)


def items_kernel(own_in, other_ref, out_ref, own_ref, ditem_ref, in_sem, out_sem):
    load = pltpu.make_async_copy(own_in, own_ref, in_sem)
    load.start()
    chips, _, block, width = ditem_ref.shape
    items = chips * 2 * block
    lane = own_ref.shape[1]
    rows = (own_ref.shape[0] - items) * lane // width
    core = lax.axis_index("c")
    load.wait()
    users = []
    for source in (own_ref, other_ref):
        parts = [
            source[items + n * rows : items + (n + 1) * rows, :] for n in range(width // lane)
        ]
        users.append(jnp.concatenate(parts, 1))
    users = jnp.concatenate(users, 0)
    grads = jnp.concatenate([own_ref[:items, :], other_ref[:items, :]], 1)
    steps = 4
    part = chips // steps
    for step in range(steps):
        at = slice(step * part, (step + 1) * part)
        some = grads[step * items // steps : (step + 1) * items // steps]
        ditem_ref[at] = dot_nn(some, users).astype(BF).reshape(part, 2, block, width)
    back = pltpu.make_async_copy(ditem_ref.at[:, core], out_ref, out_sem)
    back.start()
    back.wait()


def items_pass(own, other, chips, items, width):
    block = items // (2 * chips)
    return pl.pallas_call(
        items_kernel,
        in_specs=hbm(1) + vmem(1),
        out_specs=vmem(1)[0],
        out_shape=jax.ShapeDtypeStruct((chips, block, width), BF),
        scratch_shapes=[
            pltpu.VMEM(own.shape, BF),
            pltpu.VMEM((chips, 2, block, width), BF),
            pltpu.SemaphoreType.DMA,
            pltpu.SemaphoreType.DMA,
        ],
        compiler_params=pltpu.CompilerParams(**PARAMS),
        cost_estimate=estimate(512 * items * width, 4 * 1024 * 1024),
        name="items_pass",
    )(*in_hbm(own), other)


def join_kernel(ditem_ref, sums_ref, inv_ref, out_ref, same_ref, extra_ref, sems):
    chips, block, width = ditem_ref.shape
    first = pltpu.make_async_copy(ditem_ref, out_ref.at[:, :, :width], sems.at[0])
    first.start()
    same_ref[...] = inv_ref[...]
    row = jnp.sum(sums_ref[...], 0)[:1]
    lanes = lax.broadcasted_iota(jnp.int32, row.shape, 1)
    numerator = jnp.sum(jnp.where(lanes == 0, row, 0.0), 1, keepdims=True)
    total = jnp.sum(jnp.where(lanes == 1, row, 0.0), 1, keepdims=True)
    places = lax.broadcasted_iota(jnp.int32, (block, 128), 1)
    extra = jnp.zeros((block, 128), F32)
    for lane, piece in enumerate(in_pieces(numerator) + in_pieces(total)):
        extra = jnp.where(places == lane, piece, extra)
    extra_ref[...] = jnp.broadcast_to(extra.astype(BF)[None], extra_ref.shape)
    second = pltpu.make_async_copy(extra_ref, out_ref.at[:, :, width:], sems.at[1])
    second.start()
    first.wait()
    second.wait()


def join(d_item, sums, inv):
    chips, block, width = d_item.shape
    return pl.pallas_call(
        join_kernel,
        in_specs=vmem(3),
        out_specs=hbm(1) + vmem(1),
        out_shape=[
            pltpu.HBM((chips, block, width + 128), BF),
            jax.ShapeDtypeStruct(inv.shape, F32),
        ],
        scratch_shapes=[
            pltpu.VMEM((chips, block, 128), BF),
            pltpu.SemaphoreType.DMA((2,)),
        ],
        compiler_params=pltpu.CompilerParams(**PARAMS),
        cost_estimate=estimate(d_item.size, 4 * d_item.size),
        name="join",
    )(d_item, sums, inv)


def back_kernel(
    invd_ref, segments_ref, invo_ref, pair_in, user_in, near_in, far_in, normed_in, pre_in,
    out_ref,
    grad_ref, near_ref, far_ref, user_ref, weight_ref, normed_ref, pre_ref, sems, weight_sems,
):
    rows, width = normed_ref.shape
    items = grad_ref.shape[0]
    head = width // HEADS
    loads = [
        (pair_in.at[:items, :], grad_ref), (near_in.at[:, :, width:], near_ref),
        (far_in.at[:, :, width:], far_ref), (user_in, user_ref), (normed_in, normed_ref),
        (pre_in, pre_ref),
    ]
    loads = [pltpu.make_async_copy(p, q, sems.at[n]) for n, (p, q) in enumerate(loads)]
    into = weight_copies(near_in, far_in, weight_ref, weight_sems)
    for copy in loads[:4] + into + loads[4:]:
        copy.start()
    mask = causal_mask(segments_ref[...])
    for copy in loads[:4]:
        copy.wait()
    user = user_ref[...]
    d_user = dot_tn(grad_ref[...], unit_items(near_ref, far_ref, items))
    d_output = invo_ref[...] * (d_user - user * jnp.sum(user * d_user, 1, keepdims=True))
    for copy in into:
        copy.wait()
    d_gated = dot_nt(d_output.astype(BF), weight_ref[...].reshape(width, width))
    loads[4].wait()
    loads[5].wait()
    normed = normed_ref[...]
    gate = pre_ref[:, :width].astype(F32)
    gate_s = sigmoid(gate)
    d_normed = d_gated * (gate * gate_s)
    d_gate = d_gated * normed
    out_ref[:, :width] = d_gate * (gate_s * (1.0 + gate * (1.0 - gate_s)))
    d_mixed = invd_ref[...] * (
        d_normed
        - jnp.mean(d_normed, 1, keepdims=True)
        - normed * jnp.mean(d_normed * normed, 1, keepdims=True)
    )
    dmix_bf = d_mixed.astype(BF)
    scaling = head ** (-0.5)

    def opened(part, h):
        start = part * width + h * head
        values = pre_ref[:, start : start + head].astype(F32)
        logistic = sigmoid(values)
        slope = logistic * (1.0 + values * (1.0 - logistic))
        return (values * logistic).astype(BF), slope

    for h in range(HEADS):
        value_h, value_slope = opened(1, h)
        query_h, query_slope = opened(2, h)
        key_h, key_slope = opened(3, h)
        scores = dot_nt(query_h, key_h) * scaling
        logistic = sigmoid(scores)
        att = jnp.where(mask, scores * logistic, 0.0) * (2.0 / rows)
        dmix_h = dmix_bf[:, h * head : (h + 1) * head]
        d_att = dot_nt(dmix_h, value_h)
        d_value = dot_tn(att.astype(BF), dmix_h)
        slope = logistic * (1.0 + scores * (1.0 - logistic))
        d_scores = jnp.where(mask, d_att * slope, 0.0) * (scaling * 2.0 / rows)
        d_scores = d_scores.astype(BF)
        d_query = dot_nn(d_scores, key_h)
        d_key = dot_tn(d_scores, query_h)
        for part, grad, rate in (
            (1, d_value, value_slope), (2, d_query, query_slope), (3, d_key, key_slope)
        ):
            start = part * width + h * head
            out_ref[:, start : start + head] = grad * rate


def back_pass(inv_dev, segments, inv_out, pair, user, near, far, normed, pre):
    rows, width = normed.shape
    members, block = near.shape[:2]
    items = members * block
    return pl.pallas_call(
        back_kernel,
        in_specs=vmem(3) + hbm(6),
        out_specs=vmem(1)[0],
        out_shape=jax.ShapeDtypeStruct((rows, 4 * width), F32),
        scratch_shapes=[
            pltpu.VMEM((items, rows), BF),
            pltpu.VMEM((members, block, width // 2), BF),
            pltpu.VMEM((members, block, width // 2), BF),
            pltpu.VMEM((rows, width), F32),
            pltpu.VMEM((members, 2, block, width), BF),
            pltpu.VMEM((rows, width), F32),
            pltpu.VMEM((rows, 4 * width), BF),
            pltpu.SemaphoreType.DMA((6,)),
            pltpu.SemaphoreType.DMA((2 * PLANES,)),
        ],
        compiler_params=pltpu.CompilerParams(**PARAMS),
        cost_estimate=estimate(2 * rows * width * 2304, 8 * 1024 * 1024),
        name="back_pass",
    )(inv_dev, segments, inv_out, *in_hbm(pair, user, near, far, normed, pre))


def finish_kernel(
    got_ref, table_ref, act_ref, loss_ref, proj_out, table_out, proj_ref, dtable_ref, sems
):
    width = table_ref.shape[1]
    row = jnp.sum(got_ref[:, :, width:].astype(F32), 0)[:1]
    lanes = lax.broadcasted_iota(jnp.int32, row.shape, 1)
    numerator = jnp.sum(jnp.where(lanes < 3, row, 0.0), 1, keepdims=True)
    total = jnp.sum(jnp.where(lanes < 3, 0.0, row), 1, keepdims=True)
    share = 1.0 / total
    steps = sems.shape[0] - 1
    size = act_ref.shape[0] // steps
    out = []
    for step in range(steps):
        at = slice(step * size, (step + 1) * size)
        proj_ref[at, :] = (act_ref[at, :] * share).astype(BF)
        out.append(pltpu.make_async_copy(proj_ref.at[at, :], proj_out.at[at, :], sems.at[step]))
        out[-1].start()
    loss_ref[...] = jnp.broadcast_to(numerator * share, loss_ref.shape)
    summed = jnp.sum(got_ref[:, :, :width].astype(F32), 0)
    own = table_ref[...].astype(F32)
    inverse = lax.rsqrt(jnp.sum(own * own, 1, keepdims=True) + 1e-06)
    item = own * inverse
    inner = jnp.sum(item * summed, 1, keepdims=True)
    dtable_ref[...] = (share * inverse) * (summed - item * inner)
    out.append(pltpu.make_async_copy(dtable_ref, table_out, sems.at[steps]))
    out[-1].start()
    for copy in out:
        copy.wait()


def finish(got, table, d_act):
    rows, columns = d_act.shape
    return pl.pallas_call(
        finish_kernel,
        in_specs=vmem(3),
        out_specs=vmem(1) + hbm(2),
        out_shape=[
            jax.ShapeDtypeStruct((1, 128), F32),
            pltpu.HBM((rows, columns), BF),
            pltpu.HBM(table.shape, F32),
        ],
        scratch_shapes=[
            pltpu.VMEM((rows, columns), BF),
            pltpu.VMEM(table.shape, F32),
            pltpu.SemaphoreType.DMA((9,)),
        ],
        compiler_params=pltpu.CompilerParams(**PARAMS),
        cost_estimate=estimate(rows * columns, rows * columns * 6),
        name="finish",
    )(got, table, d_act)


def shards(
    proj, resid, send_rows, pack_rows, segments, targets, ratios, negatives, table, out_weight, topk,
    *, groups, members,
):
    width = resid.shape[1]
    mine = table.shape[0]
    with jax.named_scope("shared"):
        share = shared_blocks(table, out_weight, members)
        share = lax.all_to_all(
            share.reshape(members, mine, share.shape[1]), MEMBERS, 0, 0, tiled=True
        )
    with jax.named_scope("route"):
        send = send_blocks(send_rows, proj, resid)
        got = lax.all_to_all(
            send.reshape(members, -1, 5 * width), MEMBERS, 0, 0, tiled=True
        ).reshape(send.shape)
    with jax.named_scope("planes"):
        size = width // PLANES
        mine_part = share[:, :, :size]
        parts = [mine_part]
        for shift in SHIFTS[1:]:
            pairs = [(i, (i - shift) % groups) for i in range(groups)]
            parts.append(lax.ppermute(mine_part, "z", pairs))
        near = jnp.concatenate(parts + [share[:, :, size:]], 2)
        far = lax.ppermute(near, "c", [(0, 1), (1, 0)])
    inv_dev, inv_out, pair, sums, user, pre, normed = forward_pass(
        pack_rows, segments, got, near, far, negatives, targets, ratios, topk, 2 * groups
    )
    with jax.named_scope("sums"):
        sums = lax.all_to_all(sums, ("z", "c"), 0, 0, tiled=True)
    with jax.named_scope("items_back"):
        pair_other = lax.ppermute(pair, "c", [(0, 1), (1, 0)])
        d_item = items_pass(pair, pair_other, members // 2, members * mine, width)
        d_item, inv_out = join(d_item, sums, inv_out)
        got_item = lax.all_to_all(d_item, ("x", "y"), 0, 0, tiled=True)
    d_act = back_pass(inv_dev, segments, inv_out, pair, user, near, far, normed, pre)
    loss, d_proj, d_table = finish(got_item, table, d_act)
    return (loss[0, :1], d_proj, d_table)


def solution(mesh):
    groups, members = mesh.devices.shape
    side = 4
    fine = Mesh(
        mesh.devices.reshape(groups, side, members // (2 * side), 2), ("z", "x", "y", "c")
    )

    def body(*args):
        return shards(*args, groups=groups, members=members)

    return jax.shard_map(
        body,
        mesh=fine,
        in_specs=(
            P(EVERY, None),
            P(EVERY, None),
            P(EVERY, None),
            P(EVERY, None),
            P(EVERY, None),
            P(EVERY, None),
            P(EVERY, None),
            P("z", None),
            P(EVERY, None),
            P(MEMBERS, None),
            P(),
        ),
        out_specs=(P(), P(EVERY, None), P(EVERY, None)),
        check_vma=False,
    )
```
